256 devices in a mesh: section: 2 (over core), slab: 32 (over z_hi, y, x), dp: 4 (over z_lo).
Axes of the slice: x: 4, y: 4, z: 8 (z_hi: 2, z_lo: 4; z = z_hi * 4 + z_lo), core: 2. Of those that a mesh axis runs over, the one named last changes fastest.
Arguments:
- fields: bfloat16 [2, 64, 16, 2, 64, 256], P('section', 'slab', 'dp'), may hold values from -6 to 6
- kernels: bfloat16 [2, 2, 3, 3, 256, 256], P('section'), may hold values from -0.09375 to 0.09375
- codebook: bfloat16 [32768, 256], P('slab'), may hold values from -6 to 6
- codes: int32 [64, 16, 2, 64], P(None, 'dp'), may hold values from 0 to 32767
Outputs:
- weight_grads: float32 [2, 2, 3, 3, 256, 256], P('section')
The draws below stay inside these ranges and needn't reach their ends.
All inputs are finite; a program needn't handle non-finite values.
Results may differ from the reference program's by a relative error of at most 0.0014.
Values may be sent and summed in bfloat16 or wider, within the bound.
No kernel may reach another device: no remote copies, remote signals or barrier semaphores. Data moves between devices by JAX's collectives and lax.ppermute only.
A program may use at most 128 MiB of HBM per device.

```python
import math
import jax
import jax.numpy as jnp
from jax import lax

C = 256
FRAMES = 2
VOCAB = 32768
SIDE = 64
MB = 16


def with_ends(result, own_key, low, top_value):
    dims = result.shape
    place = [jax.random.randint(jax.random.fold_in(own_key, axis), (), 0, dims[axis]) for axis in range(len(dims))]
    result = result.at[tuple(place)].set(low)
    longest = dims.index(max(dims))
    place[longest] = (place[longest] + 1) % dims[longest]
    return result.at[tuple(place)].set(top_value)


def levels(rng, shape, shards, low, high):
    def one(axis_at, parts):
        draws = jax.random.uniform(jax.random.fold_in(jax.random.fold_in(rng, 6), axis_at), (parts,), jnp.float32, low / len(shards), high / len(shards))
        return jnp.repeat(jnp.exp(draws), shape[axis_at] // parts).reshape((-1,) + (1,) * (len(shape) - axis_at - 1))

    loudness = one(*shards[0])
    for cut in shards[1:]:
        loudness = loudness * one(*cut)
    return loudness


def bell_draw(own_key, dims, spread, limit, cuts=(), kind=jnp.bfloat16):
    values = jax.random.normal(own_key, dims, jnp.float32) * spread
    if len(cuts) > 0:
        values = levels(own_key, dims, cuts, -0.22, 0.18) * values
    return jnp.clip(values, min=-limit, max=limit).astype(kind)


def setup_inputs(seed: int = 0) -> dict:
    keys = jax.random.split(jax.random.key(seed), 5)
    return {
        "fields": bell_draw(keys[0], (2, SIDE, MB, FRAMES, SIDE, C), 1.0, 6.0, ((0, 2), (1, 32), (2, 4))),
        "kernels": bell_draw(keys[1], (2, 2, 3, 3, C, C), (18 * C) ** -0.5, 0.09375, ((0, 2),)),
        "codebook": bell_draw(keys[2], (VOCAB, C), 1.0, 6.0, ((0, 32),)),
        "codes": with_ends(jax.random.randint(keys[3], (SIDE, MB, FRAMES, SIDE), 0, VOCAB), jax.random.fold_in(keys[3], 1), 0, VOCAB - 1).astype(jnp.int32),
    }


COMMIT = 0.5

def silu_slope(pre_act):
    sig = jax.nn.sigmoid(pre_act)
    return sig * (1.0 + pre_act * (1.0 - sig))

def columns(padded, offset_sign, row_count, frame_count, across):
    pieces = []
    for tap_t in range(2):
        for tap_r in range(3):
            for tap_q in range(3):
                shift_t = 1 + offset_sign * (tap_t - 1)
                shift_r = 1 + offset_sign * (tap_r - 1)
                shift_q = 1 + offset_sign * (tap_q - 1)
                pieces.append(padded[shift_r:shift_r + row_count, :, shift_t:shift_t + frame_count, shift_q:shift_q + across, :])
    return jnp.concatenate(pieces, axis=-1)

def padded_cols(field, offset_sign):
    padded = jnp.pad(field, ((1, 1), (0, 0), (1, 1), (1, 1), (0, 0)))
    tap_cols = columns(padded, offset_sign, field.shape[0], field.shape[2], field.shape[3])
    return tap_cols.reshape(-1, tap_cols.shape[-1])

def convolve(field, kernel):
    width_c = kernel.shape[-1]
    flat_cols = padded_cols(field, 1)
    return jnp.dot(flat_cols, kernel.reshape(-1, width_c), preferred_element_type=jnp.float32).reshape(field.shape)

def adjoint(grad, kernel):
    width_c = kernel.shape[-1]
    flat_cols = padded_cols(grad, -1)
    kernel_t = jnp.swapaxes(kernel, -1, -2).reshape(-1, width_c)
    return jnp.dot(flat_cols, kernel_t, preferred_element_type=jnp.float32).reshape(grad.shape)

def weight_grad(field, grad):
    width_c = field.shape[-1]
    flat_cols = padded_cols(field, 1)
    summed = lax.dot_general(flat_cols, grad.reshape(-1, width_c), (((0,), (0,)), ((), ())), preferred_element_type=jnp.float32)
    return summed.reshape(2, 3, 3, width_c, width_c)

def reference(fields, kernels, codebook, codes):
    enc_in = fields[0]
    dec_cot = fields[1]
    quant = jnp.take(codebook, codes, axis=0)
    latent_enc = convolve(enc_in, kernels[0])
    quant_dec = jnp.transpose(quant, (3, 1, 2, 0, 4))
    pre_dec = convolve(quant_dec, kernels[1])
    dec_grad = (dec_cot.astype(jnp.float32) * silu_slope(pre_dec)).astype(jnp.bfloat16)
    back_dec = adjoint(dec_grad, kernels[1]).astype(jnp.bfloat16)
    back_enc = jnp.transpose(back_dec, (3, 1, 2, 0, 4))
    enc_grad = (back_enc.astype(jnp.float32) + COMMIT * (latent_enc - quant.astype(jnp.float32))).astype(jnp.bfloat16)
    grad_enc = weight_grad(enc_in, enc_grad)
    grad_dec = weight_grad(quant_dec, dec_grad)
    norm_factor = math.sqrt(SIDE * SIDE * MB * FRAMES)
    return jnp.stack([grad_enc, grad_dec]) / norm_factor
```

```python
import math

import jax
import jax.numpy as jnp
from jax import lax
from jax.sharding import Mesh, PartitionSpec as P

COMMIT = 0.5
SLAB = ("zh", "y", "x")
Z = ("zh", "dp")
F32 = jnp.float32
BF16 = jnp.bfloat16
F16 = jnp.float16
TINY = 2.0**-100


def silu_slope(pre_act):
    sig = jax.nn.sigmoid(pre_act)
    return sig * (1.0 + pre_act * (1.0 - sig))


def columns(padded, offset_sign, row_count, frame_count, across):
    pieces = []
    for tap_t in range(2):
        for tap_r in range(3):
            for tap_q in range(3):
                shift_t = 1 + offset_sign * (tap_t - 1)
                shift_r = 1 + offset_sign * (tap_r - 1)
                shift_q = 1 + offset_sign * (tap_q - 1)
                pieces.append(
                    padded[
                        shift_r : shift_r + row_count,
                        :,
                        shift_t : shift_t + frame_count,
                        shift_q : shift_q + across,
                        :,
                    ]
                )
    return jnp.concatenate(pieces, axis=-1)


def tap_columns(rimmed, offset_sign):
    rows, _, frames, across, channels = rimmed.shape
    padded = jnp.pad(rimmed, ((0, 0), (0, 0), (1, 1), (1, 1), (0, 0)))
    return columns(padded, offset_sign, rows - 2, frames, across).reshape(-1, 18 * channels)


def neighbours(lower, upper):
    count = lax.axis_size(SLAB)
    above = lax.ppermute(lower, SLAB, [(i, i + 1) for i in range(count - 1)])
    below = lax.ppermute(upper, SLAB, [(i + 1, i) for i in range(count - 1)])
    return above, below


def exchange(cells, axes):
    return lax.all_to_all(cells, axes, split_axis=0, concat_axis=0, tiled=True)


def on_device(fields, kernels, codebook, codes):
    section_id = lax.axis_index("section")
    decoder = section_id == 1
    slab_id = lax.axis_index(SLAB)
    slabs = lax.axis_size(SLAB)
    own_field = fields[0]
    kernel = kernels[0]
    kernel = jnp.where(decoder, jnp.swapaxes(kernel, 1, 2), kernel)
    row_count, batch_count, frame_count, across, channels = own_field.shape
    book = codebook.shape[0]
    positions = row_count * batch_count * frame_count * across
    slots = max(16, 2 * positions // slabs)

    edge = jnp.full((1,) + codes.shape[1:], -1, codes.dtype)
    shifted = jnp.concatenate([edge, codes, edge], axis=0)
    pairs = lax.dynamic_slice_in_dim(shifted, section_id * row_count, codes.shape[0], 0)
    wanted = pairs.reshape(slabs, positions)
    owner = jnp.where(wanted >= 0, wanted // book, -1)
    before = (
        lax.broadcasted_iota(jnp.int32, (positions, positions), 0)
        < lax.broadcasted_iota(jnp.int32, (positions, positions), 1)
    ).astype(BF16)

    mine = owner == slab_id
    rank = jnp.dot(mine.astype(BF16), before, preferred_element_type=F32).astype(jnp.int32)
    rank = jnp.where(mine, rank, -1)
    local = wanted - slab_id * book
    slot_ids = lax.broadcasted_iota(jnp.int32, (1, slots, 1), 1)
    asked = jnp.sum(jnp.where(rank[:, None, :] == slot_ids, local[:, None, :], 0), axis=-1)
    picks = (
        asked.reshape(-1, 1) == lax.broadcasted_iota(jnp.int32, (1, book), 1)
    ).astype(BF16)
    words = jnp.dot(picks, codebook, preferred_element_type=F32).astype(BF16)
    words = words.reshape(slabs, slots, channels)

    turned = jnp.transpose(own_field, (3, 1, 2, 0, 4)).reshape(slabs, -1, channels)
    arrived = exchange(jnp.concatenate([words, turned], axis=1), SLAB)
    looked = arrived[:, :slots].reshape(slabs * slots, channels)
    cotangent = arrived[:, slots:].reshape(
        slabs, row_count, batch_count, frame_count, row_count, channels
    )
    cotangent = jnp.transpose(cotangent, (1, 2, 3, 0, 4, 5)).reshape(positions, channels)

    own_wanted = lax.dynamic_index_in_dim(wanted, slab_id, 0, keepdims=False)
    own_owner = lax.dynamic_index_in_dim(owner, slab_id, 0, keepdims=False)
    from_each = own_owner[None, :] == lax.broadcasted_iota(jnp.int32, (slabs, 1), 0)
    place = jnp.dot(from_each.astype(BF16), before, preferred_element_type=F32).astype(jnp.int32)
    place = jnp.sum(jnp.where(from_each, place, 0), axis=0)
    place = jnp.where(own_wanted >= 0, own_owner * slots + place, -1)
    gather = (
        place[:, None] == lax.broadcasted_iota(jnp.int32, (1, slabs * slots), 1)
    ).astype(BF16)
    fast = jnp.dot(gather, looked, preferred_element_type=F32).astype(BF16)

    every_owner = jnp.where(shifted >= 0, shifted // book, -1).reshape(slabs + 1, 1, positions)
    counts = jnp.sum(
        (every_owner == lax.broadcasted_iota(jnp.int32, (1, slabs, 1), 1)).astype(F32), axis=-1
    )
    crowded = jnp.full((lax.axis_size("dp"), 8, 128), jnp.max(counts) - slots)
    crowded = jnp.max(exchange(crowded, "dp")) > 0

    def whole_book(_):
        every = lax.all_gather(codebook, SLAB, axis=0, tiled=True)
        taken = jnp.take(every, jnp.maximum(own_wanted, 0), axis=0)
        return jnp.where(own_wanted[:, None] >= 0, taken, 0).astype(BF16)

    pair = lax.cond(crowded, whole_book, lambda quick: quick, fast)
    other = lax.ppermute(pair, "section", [(0, 1), (1, 0)])
    quant = jnp.concatenate(
        [jnp.where(decoder, other, pair), jnp.where(decoder, pair, other)], axis=0
    ).reshape(row_count + 2, batch_count, frame_count, across, channels)
    above, below = neighbours(own_field[-1:], own_field[:1])
    rimmed = jnp.concatenate([above, own_field, below], axis=0)
    tap_cols = tap_columns(jnp.where(decoder, quant, rimmed), 1)
    pre_act = jnp.dot(tap_cols, kernel.reshape(-1, channels), preferred_element_type=F32)

    dec_grad = (cotangent.astype(F32) * silu_slope(pre_act)).astype(BF16)
    shaped = dec_grad.reshape(own_field.shape)
    above, below = neighbours(shaped[-1:], shaped[:1])
    grad_cols = tap_columns(jnp.concatenate([above, shaped, below], axis=0), -1)
    kernel_t = jnp.swapaxes(kernel, -1, -2).reshape(-1, channels)
    back_dec = jnp.dot(grad_cols, kernel_t, preferred_element_type=F32).astype(BF16)
    returned = lax.ppermute(back_dec, "section", [(1, 0)])
    own_quant = quant[1:-1].reshape(positions, channels)
    enc_grad = (
        returned.astype(F32) + COMMIT * (pre_act - own_quant.astype(F32))
    ).astype(BF16)
    weight_side = jnp.where(decoder, dec_grad, enc_grad)
    partial_grad = lax.dot_general(
        tap_cols, weight_side, (((0,), (0,)), ((), ())), preferred_element_type=F32
    )

    total = (
        row_count * slabs * across * batch_count * lax.axis_size("dp") * frame_count
    )
    nx, ny, nz = lax.axis_size("x"), lax.axis_size("y"), lax.axis_size(Z)
    ci = channels // nx // ny
    part = partial_grad.reshape(18, nx, ny * ci * channels // 128, 128)
    part = jnp.transpose(part, (1, 0, 2, 3))
    part = jnp.sum(exchange(part, "x").reshape(nx, 18, ny, -1, 128), axis=0)
    part = jnp.transpose(part, (1, 0, 2, 3))
    part = jnp.sum(exchange(part, "y"), axis=0)
    part = jnp.sum(exchange(part.reshape(nz, -1, 128), Z).reshape(nz, -1, 128), axis=0)
    part = part / math.sqrt(total)

    def collect(piece, axes, count):
        return exchange(jnp.broadcast_to(piece[None], (count,) + piece.shape), axes)

    exponent = jnp.clip(jnp.ceil(jnp.log2(jnp.max(jnp.abs(part)) + TINY)), -100.0, 120.0)
    coded = (part * jnp.exp2(-exponent)).astype(F16)
    share = jnp.concatenate([coded, jnp.full((8, 128), exponent).astype(F16)], axis=0)
    share = collect(share, Z, nz)
    share = collect(share, "y", ny)
    share = collect(share, "x", nx)
    scale = jnp.exp2(share[:, :, :, -1:, :1].astype(F32))
    share = share[:, :, :, :-8].astype(F32) * scale
    share = share.reshape(nx, ny, 18, -1, 128)
    share = jnp.transpose(share, (2, 0, 1, 3, 4)).reshape(2, 3, 3, channels, channels)
    share = jnp.where(decoder, jnp.swapaxes(share, 1, 2), share)
    return share[None]


def solution(mesh):
    sections, slabs, dps = (mesh.shape[a] for a in ("section", "slab", "dp"))
    nx = 4 if slabs >= 16 else 2
    inner = Mesh(
        mesh.devices.reshape(sections, slabs // (nx * nx), nx, nx, dps),
        ("section", "zh", "y", "x", "dp"),
    )
    placed = (
        P("section", SLAB, "dp", None, None, None),
        P("section", None, None, None, None, None),
        P(SLAB, None),
        P(None, "dp", None, None),
    )
    return jax.shard_map(
        on_device,
        mesh=inner,
        in_specs=placed,
        out_specs=P("section", None, None, None, None, None),
        check_vma=False,
    )
```

```python
import math

import jax
import jax.numpy as jnp
from jax import lax
from jax.experimental import pallas as pl
from jax.experimental.pallas import tpu as pltpu
from jax.sharding import Mesh, PartitionSpec as P

COMMIT = 0.5
SLAB = ("zh", "y", "x")
Z = ("zh", "dp")
F32 = jnp.float32
BF16 = jnp.bfloat16
I16 = jnp.int16
TINY = 2.0**-100
STEPS = 32000.0
VMEM_LIMIT = 48 * 1024 * 1024


def silu_slope(pre_act):
    sig = jax.nn.sigmoid(pre_act)
    return sig * (1.0 + pre_act * (1.0 - sig))


def columns(padded, offset_sign, row_count, frame_count, across):
    pieces = []
    for tap_t in range(2):
        for tap_r in range(3):
            for tap_q in range(3):
                shift_t = 1 + offset_sign * (tap_t - 1)
                shift_r = 1 + offset_sign * (tap_r - 1)
                shift_q = 1 + offset_sign * (tap_q - 1)
                pieces.append(
                    padded[
                        shift_r : shift_r + row_count,
                        :,
                        shift_t : shift_t + frame_count,
                        shift_q : shift_q + across,
                        :,
                    ]
                )
    return jnp.concatenate(pieces, axis=-1)


def tap_columns(rimmed, offset_sign):
    rows, _, frames, across, channels = rimmed.shape
    padded = jnp.pad(rimmed, ((0, 0), (0, 0), (1, 1), (1, 1), (0, 0)))
    return columns(padded, offset_sign, rows - 2, frames, across).reshape(-1, 18 * channels)


def neighbours(lower, upper):
    count = lax.axis_size(SLAB)
    above = lax.ppermute(lower, SLAB, [(i, i + 1) for i in range(count - 1)])
    below = lax.ppermute(upper, SLAB, [(i + 1, i) for i in range(count - 1)])
    return above, below


def exchange(cells, axes):
    return lax.all_to_all(cells, axes, split_axis=0, concat_axis=0, tiled=True)


def coded(values):
    top = jnp.max(jnp.abs(values), axis=tuple(range(values.ndim)), keepdims=True)
    exponent = jnp.ceil(jnp.log2(top + TINY))
    return jnp.round(values * (jnp.exp2(-exponent) * STEPS)), exponent


def decoded_scale(exponents):
    return jnp.exp2(exponents.astype(F32)) * (1.0 / STEPS)


def framed(piece):
    steps, exponent = coded(piece)
    tail = jnp.broadcast_to(exponent, (8, 128))
    return jnp.concatenate([steps, tail], axis=0).astype(I16)


def unframed(rows):
    wide = rows.astype(F32)
    return wide[:-8] * (jnp.exp2(wide[-1:]) * (1.0 / STEPS))


def pack_plane(grads, parts):
    taps, ins, outs = grads.shape
    size = ins // parts

    def body(grads_ref, packed_ref):
        steps, exponent = coded(grads_ref[...])
        packed_ref[0, :taps] = steps.astype(I16)
        packed_ref[0, taps] = jnp.broadcast_to(exponent[0], (size, outs)).astype(I16)

    return pl.pallas_call(
        body,
        grid=(parts,),
        in_specs=[pl.BlockSpec((taps, size, outs), lambda k: (0, k, 0))],
        out_specs=pl.BlockSpec((1, taps + 1, size, outs), lambda k: (k, 0, 0, 0)),
        out_shape=jax.ShapeDtypeStruct((parts, taps + 1, size, outs), I16),
    )(grads)


def sum_plane(packed, pieces):
    senders, taps, size, outs = packed.shape
    taps = taps - 1
    half = taps // 2

    def body(packed_ref, framed_ref, total):
        scales = [decoded_scale(packed_ref[s, taps])[:1, :1] for s in range(senders)]
        for tap in range(taps):
            acc = packed_ref[0, tap].astype(F32) * scales[0]
            for s in range(1, senders):
                acc += packed_ref[s, tap].astype(F32) * scales[s]
            total[tap] = acc
        place = 0
        for frame in range(2):
            for oct_ in range(size // 8):
                for lane in range(outs // 128):
                    piece = total[
                        frame * half : (frame + 1) * half,
                        oct_ * 8 : oct_ * 8 + 8,
                        lane * 128 : lane * 128 + 128,
                    ]
                    framed_ref[place] = framed(piece.reshape(half * 8, 128))
                    place += 1

    return pl.pallas_call(
        body,
        out_shape=jax.ShapeDtypeStruct((pieces, half * 8 + 8, 128), I16),
        scratch_shapes=[pltpu.VMEM((taps, size, outs), F32)],
        compiler_params=pltpu.CompilerParams(vmem_limit_bytes=VMEM_LIMIT),
    )(packed)


def sum_line(framed_parts, factor):
    def body(parts_ref, out_ref):
        acc = unframed(parts_ref[0])
        for s in range(1, framed_parts.shape[0]):
            acc += unframed(parts_ref[s])
        result = framed(acc * factor)
        for s in range(framed_parts.shape[0]):
            out_ref[s] = result

    return pl.pallas_call(
        body, out_shape=jax.ShapeDtypeStruct(framed_parts.shape, I16)
    )(framed_parts)


def unpack(plane, section_id, channels):
    parts, pieces, rows, _ = plane.shape
    size = channels // parts

    def body(section_ref, plane_ref, out_ref):
        def write(turned):
            place = 0
            for frame in range(2):
                for oct_ in range(size // 8):
                    for lane in range(channels // 128):
                        piece = unframed(plane_ref[0, place]).reshape(3, 3, 8, 128)
                        for r in range(3):
                            for q in range(3):
                                out_ref[
                                    frame,
                                    q if turned else r,
                                    r if turned else q,
                                    oct_ * 8 : oct_ * 8 + 8,
                                    lane * 128 : lane * 128 + 128,
                                ] = piece[r, q]
                        place += 1

        @pl.when(section_ref[0] == 0)
        def _():
            write(False)

        @pl.when(section_ref[0] == 1)
        def _():
            write(True)

    return pl.pallas_call(
        body,
        grid_spec=pltpu.PrefetchScalarGridSpec(
            num_scalar_prefetch=1,
            grid=(parts,),
            in_specs=[pl.BlockSpec((1, pieces, rows, 128), lambda k, _: (k, 0, 0, 0))],
            out_specs=pl.BlockSpec((2, 3, 3, size, channels), lambda k, _: (0, 0, 0, k, 0)),
        ),
        out_shape=jax.ShapeDtypeStruct((2, 3, 3, channels, channels), F32),
    )(section_id.reshape(1).astype(jnp.int32), plane)


def on_device(fields, kernels, codebook, codes):
    section_id = lax.axis_index("section")
    decoder = section_id == 1
    slab_id = lax.axis_index(SLAB)
    slabs = lax.axis_size(SLAB)
    own_field = fields[0]
    kernel = kernels[0]
    kernel = jnp.where(decoder, jnp.swapaxes(kernel, 1, 2), kernel)
    row_count, batch_count, frame_count, across, channels = own_field.shape
    book = codebook.shape[0]
    positions = row_count * batch_count * frame_count * across
    slots = max(16, 2 * positions // slabs)

    edge = jnp.full((1,) + codes.shape[1:], -1, codes.dtype)
    shifted = jnp.concatenate([edge, codes, edge], axis=0)
    pairs = lax.dynamic_slice_in_dim(shifted, section_id * row_count, codes.shape[0], 0)
    wanted = pairs.reshape(slabs, positions)
    owner = jnp.where(wanted >= 0, wanted // book, -1)
    before = (
        lax.broadcasted_iota(jnp.int32, (positions, positions), 0)
        < lax.broadcasted_iota(jnp.int32, (positions, positions), 1)
    ).astype(BF16)

    mine = owner == slab_id
    rank = jnp.dot(mine.astype(BF16), before, preferred_element_type=F32).astype(jnp.int32)
    rank = jnp.where(mine, rank, -1)
    local = wanted - slab_id * book
    slot_ids = lax.broadcasted_iota(jnp.int32, (1, slots, 1), 1)
    asked = jnp.sum(jnp.where(rank[:, None, :] == slot_ids, local[:, None, :], 0), axis=-1)
    picks = (
        asked.reshape(-1, 1) == lax.broadcasted_iota(jnp.int32, (1, book), 1)
    ).astype(BF16)
    words = jnp.dot(picks, codebook, preferred_element_type=F32).astype(BF16)
    words = words.reshape(slabs, slots, channels)

    turned = jnp.transpose(own_field, (3, 1, 2, 0, 4)).reshape(slabs, -1, channels)
    arrived = exchange(jnp.concatenate([words, turned], axis=1), SLAB)
    looked = arrived[:, :slots].reshape(slabs * slots, channels)
    cotangent = arrived[:, slots:].reshape(
        slabs, row_count, batch_count, frame_count, row_count, channels
    )
    cotangent = jnp.transpose(cotangent, (1, 2, 3, 0, 4, 5)).reshape(positions, channels)

    own_wanted = lax.dynamic_index_in_dim(wanted, slab_id, 0, keepdims=False)
    own_owner = lax.dynamic_index_in_dim(owner, slab_id, 0, keepdims=False)
    from_each = own_owner[None, :] == lax.broadcasted_iota(jnp.int32, (slabs, 1), 0)
    place = jnp.dot(from_each.astype(BF16), before, preferred_element_type=F32).astype(jnp.int32)
    place = jnp.sum(jnp.where(from_each, place, 0), axis=0)
    place = jnp.where(own_wanted >= 0, own_owner * slots + place, -1)
    gather = (
        place[:, None] == lax.broadcasted_iota(jnp.int32, (1, slabs * slots), 1)
    ).astype(BF16)
    fast = jnp.dot(gather, looked, preferred_element_type=F32).astype(BF16)

    every_owner = jnp.where(shifted >= 0, shifted // book, -1).reshape(slabs + 1, 1, positions)
    counts = jnp.sum(
        (every_owner == lax.broadcasted_iota(jnp.int32, (1, slabs, 1), 1)).astype(F32), axis=-1
    )
    crowded = jnp.full((lax.axis_size("dp"), 8, 128), jnp.max(counts) - slots)
    crowded = jnp.max(exchange(crowded, "dp")) > 0

    def whole_book(_):
        every = lax.all_gather(codebook, SLAB, axis=0, tiled=True)
        taken = jnp.take(every, jnp.maximum(own_wanted, 0), axis=0)
        return jnp.where(own_wanted[:, None] >= 0, taken, 0).astype(BF16)

    pair = lax.cond(crowded, whole_book, lambda quick: quick, fast)
    other = lax.ppermute(pair, "section", [(0, 1), (1, 0)])
    quant = jnp.concatenate(
        [jnp.where(decoder, other, pair), jnp.where(decoder, pair, other)], axis=0
    ).reshape(row_count + 2, batch_count, frame_count, across, channels)
    above, below = neighbours(own_field[-1:], own_field[:1])
    rimmed = jnp.concatenate([above, own_field, below], axis=0)
    tap_cols = tap_columns(jnp.where(decoder, quant, rimmed), 1)
    pre_act = jnp.dot(tap_cols, kernel.reshape(-1, channels), preferred_element_type=F32)

    dec_grad = (cotangent.astype(F32) * silu_slope(pre_act)).astype(BF16)
    shaped = dec_grad.reshape(own_field.shape)
    above, below = neighbours(shaped[-1:], shaped[:1])
    grad_cols = tap_columns(jnp.concatenate([above, shaped, below], axis=0), -1)
    kernel_t = jnp.swapaxes(kernel, -1, -2).reshape(-1, channels)
    back_dec = jnp.dot(grad_cols, kernel_t, preferred_element_type=F32).astype(BF16)
    returned = lax.ppermute(back_dec, "section", [(1, 0)])
    own_quant = quant[1:-1].reshape(positions, channels)
    enc_grad = (
        returned.astype(F32) + COMMIT * (pre_act - own_quant.astype(F32))
    ).astype(BF16)
    weight_side = jnp.where(decoder, dec_grad, enc_grad)
    partial_grad = lax.dot_general(
        tap_cols, weight_side, (((0,), (0,)), ((), ())), preferred_element_type=F32
    )

    total = (
        row_count * slabs * across * batch_count * lax.axis_size("dp") * frame_count
    )
    nx, ny, nz = lax.axis_size("x"), lax.axis_size("y"), lax.axis_size(Z)
    plane = exchange(pack_plane(partial_grad.reshape(18, channels, channels), nx * ny), ("y", "x"))
    line = exchange(sum_plane(plane, nz), Z)
    line = exchange(sum_line(line, 1.0 / math.sqrt(total)), Z)
    plane = exchange(jnp.broadcast_to(line[None], (nx * ny,) + line.shape), ("y", "x"))
    return unpack(plane, section_id, channels)[None]


def solution(mesh):
    sections, slabs, dps = (mesh.shape[a] for a in ("section", "slab", "dp"))
    nx = 4 if slabs >= 16 else 2
    inner = Mesh(
        mesh.devices.reshape(sections, slabs // (nx * nx), nx, nx, dps),
        ("section", "zh", "y", "x", "dp"),
    )
    placed = (
        P("section", SLAB, "dp", None, None, None),
        P("section", None, None, None, None, None),
        P(SLAB, None),
        P(None, "dp", None, None),
    )
    return jax.shard_map(
        on_device,
        mesh=inner,
        in_specs=placed,
        out_specs=P("section", None, None, None, None, None),
        check_vma=False,
    )
```

```python
import math

import jax
import jax.numpy as jnp
from jax import lax
from jax.experimental import pallas as pl
from jax.experimental.pallas import tpu as pltpu
from jax.sharding import Mesh, PartitionSpec as P

COMMIT = 0.5
SLAB = ("zh", "y", "x")
Z = ("zh", "dp")
F32 = jnp.float32
BF16 = jnp.bfloat16
I16 = jnp.int16
TINY = 2.0**-100
STEPS = 32000.0
VMEM_LIMIT = 48 * 1024 * 1024


def silu_slope(pre_act):
    sig = jax.nn.sigmoid(pre_act)
    return sig * (1.0 + pre_act * (1.0 - sig))


def neighbours(lower, upper):
    count = lax.axis_size(SLAB)
    above = lax.ppermute(lower, SLAB, [(i, i + 1) for i in range(count - 1)])
    below = lax.ppermute(upper, SLAB, [(i + 1, i) for i in range(count - 1)])
    return above, below


def exchange(cells, axes):
    return lax.all_to_all(cells, axes, split_axis=0, concat_axis=0, tiled=True)


def coded(values):
    top = jnp.max(jnp.abs(values), axis=tuple(range(values.ndim)), keepdims=True)
    exponent = jnp.ceil(jnp.log2(top + TINY))
    return jnp.round(values * (jnp.exp2(-exponent) * STEPS)), exponent


def decoded_scale(exponents):
    return jnp.exp2(exponents.astype(F32)) * (1.0 / STEPS)


def framed(piece):
    steps, exponent = coded(piece)
    tail = jnp.broadcast_to(exponent, (8, 128))
    return jnp.concatenate([steps, tail], axis=0).astype(I16)


def unframed(rows):
    wide = rows.astype(F32)
    return wide[:-8] * (jnp.exp2(wide[-1:]) * (1.0 / STEPS))


def shifted_columns(block, across, tap):
    if tap == 1:
        return block
    count = block.shape[0]
    wide = block.astype(F32)
    column = lax.broadcasted_iota(jnp.int32, block.shape, 0) % across
    if tap == 0:
        wide = jnp.where(column == 0, 0.0, pltpu.roll(wide, 1, 0))
    else:
        wide = jnp.where(column == across - 1, 0.0, pltpu.roll(wide, count - 1, 0))
    return wide.astype(block.dtype)


def call(body, outs, *args, flops=0, scratch=()):
    size = sum(math.prod(a.shape) * a.dtype.itemsize for a in args) + sum(
        math.prod(o.shape) * o.dtype.itemsize for o in outs
    )
    return pl.pallas_call(
        body,
        in_specs=[pl.BlockSpec(memory_space=pltpu.SMEM)]
        + [pl.BlockSpec(memory_space=pltpu.VMEM)] * (len(args) - 1),
        out_specs=[pl.BlockSpec(memory_space=pltpu.VMEM)] * len(outs),
        out_shape=list(outs),
        scratch_shapes=list(scratch),
        cost_estimate=pl.CostEstimate(flops=flops, bytes_accessed=size, transcendentals=0),
        compiler_params=pltpu.CompilerParams(vmem_limit_bytes=VMEM_LIMIT),
    )(*args)


def shift_source(section, pair, other, own, above, below, across):
    frames, rows, count, channels = own.shape

    def body(section_ref, pair_ref, other_ref, own_ref, above_ref, below_ref, out_ref):
        def write(frame, row, block):
            for tap in range(3):
                out_ref[tap, frame, row] = shifted_columns(block, across, tap)

        @pl.when(section_ref[0] == 0)
        def _():
            for frame in range(frames):
                write(frame, 0, above_ref[frame])
                for row in range(rows):
                    write(frame, row + 1, own_ref[frame, row])
                write(frame, rows + 1, below_ref[frame])

        @pl.when(section_ref[0] == 1)
        def _():
            for frame in range(frames):
                for row in range(2):
                    write(frame, row, other_ref[frame, row])
                    write(frame, row + 2, pair_ref[frame, row])

    out = jax.ShapeDtypeStruct((3, frames, rows + 2, count, channels), BF16)
    return call(body, [out], section, pair, other, own, above, below)[0]


def turn_source(section, source):
    taps, frames, rows, count, channels = source.shape

    def body(section_ref, source_ref, out_ref):
        for tap in range(taps):
            for frame in range(frames):
                for row in range(rows):
                    start = (frame * rows + row) * count
                    out_ref[tap, :, start : start + count] = source_ref[tap, frame, row].T

    out = jax.ShapeDtypeStruct((taps, channels, frames * rows * count), BF16)
    return call(body, [out], section, source)[0]


def tap_index(section_ref, row_tap, column_tap):
    decoder = section_ref[0] == 1
    return jnp.where(decoder, column_tap, row_tap), jnp.where(decoder, row_tap, column_tap)


def convolve(section, source, kernel, cotangent):
    _, frames, rimmed, count, channels = source.shape
    rows = rimmed - 2
    span = rows * count

    def body(section_ref, source_ref, kernel_ref, cot_ref, pre_ref, grad_ref):
        for frame in range(frames):
            acc = jnp.zeros((span, channels), F32)
            for r in range(3):
                for q in range(3):
                    i, j = tap_index(section_ref, r, q)
                    for back in range(frame + 1):
                        cells = source_ref[q, frame - back, r : r + rows].reshape(span, channels)
                        acc += jnp.dot(
                            cells, kernel_ref[1 - back, i, j], preferred_element_type=F32
                        )
            pre_ref[frame] = acc
            grad_ref[frame] = (cot_ref[frame].astype(F32) * silu_slope(acc)).astype(BF16)

    shape = (frames, span, channels)
    return call(
        body,
        [jax.ShapeDtypeStruct(shape, F32), jax.ShapeDtypeStruct(shape, BF16)],
        section,
        source,
        kernel,
        cotangent,
        flops=54 * span * channels * channels,
    )


def convolve_back(section, grad, above, below, kernel, across):
    frames, rows, count, channels = grad.shape
    span = rows * count

    def body(section_ref, grad_ref, above_ref, below_ref, kernel_ref, out_ref, shifted):
        for frame in range(frames):
            blocks = [above_ref[frame]] + [grad_ref[frame, r] for r in range(rows)]
            for row, block in enumerate(blocks + [below_ref[frame]]):
                for tap in range(3):
                    shifted[tap, frame, row] = shifted_columns(block, across, tap)
        for frame in range(frames):
            acc = jnp.zeros((span, channels), F32)
            for r in range(3):
                for q in range(3):
                    i, j = tap_index(section_ref, r, q)
                    for ahead in range(frames - frame):
                        cells = shifted[2 - q, frame + ahead, 2 - r : 2 - r + rows]
                        acc += lax.dot_general(
                            cells.reshape(span, channels),
                            kernel_ref[1 - ahead, i, j],
                            (((1,), (1,)), ((), ())),
                            preferred_element_type=F32,
                        )
            out_ref[frame] = acc.astype(BF16).reshape(rows, count, channels)

    return call(
        body,
        [jax.ShapeDtypeStruct(grad.shape, BF16)],
        section,
        grad,
        above,
        below,
        kernel,
        flops=54 * span * channels * channels,
        scratch=[pltpu.VMEM((3, frames, rows + 2, count, channels), BF16)],
    )[0]


def kernel_grads(section, turned, pre_act, dec_grad, returned, pair, other, parts):
    _, channels, _ = turned.shape
    frames, rows, count, _ = returned.shape
    span = rows * count
    size = channels // parts

    def body(
        section_ref, turned_ref, pre_ref, dec_ref, returned_ref, pair_ref, other_ref,
        out_ref, side, grads,
    ):
        @pl.when(section_ref[0] == 0)
        def _():
            for frame in range(frames):
                for row, quant in enumerate((pair_ref[frame, 1], other_ref[frame, 0])):
                    at = slice(row * count, (row + 1) * count)
                    side[frame, at] = (
                        returned_ref[frame, row].astype(F32)
                        + COMMIT * (pre_ref[frame, at] - quant.astype(F32))
                    ).astype(BF16)

        @pl.when(section_ref[0] == 1)
        def _():
            side[...] = dec_ref[...]

        top = jnp.zeros((8, channels), F32)
        for r in range(3):
            for q in range(3):
                i, j = tap_index(section_ref, r, q)
                tap = i * 3 + j
                first = turned_ref[q, :, r * count : r * count + span]
                start = (rows + 2 + r) * count
                second = turned_ref[q, :, start : start + span]
                late = jnp.dot(first, side[1], preferred_element_type=F32)
                same = jnp.dot(first, side[0], preferred_element_type=F32)
                same += jnp.dot(second, side[1], preferred_element_type=F32)
                for at, values in ((tap, late), (9 + tap, same)):
                    grads[at] = values
                    seen = jnp.max(jnp.abs(values).reshape(-1, 8, channels), axis=0)
                    top = jnp.maximum(top, seen)
        exponent = jnp.ceil(jnp.log2(jnp.max(top, axis=(0, 1), keepdims=True) + TINY))
        factor = jnp.exp2(-exponent) * STEPS

        @pl.loop(0, 18)
        def _(tap):
            steps = jnp.round(grads[tap] * factor).astype(I16)
            out_ref[:, tap] = steps.reshape(parts, size, channels)

        tail = jnp.broadcast_to(exponent, (size, channels)).astype(I16)
        for part in range(parts):
            out_ref[part, 18] = tail

    return call(
        body,
        [jax.ShapeDtypeStruct((parts, 19, size, channels), I16)],
        section,
        turned,
        pre_act,
        dec_grad,
        returned,
        pair,
        other,
        flops=54 * span * channels * channels,
        scratch=[
            pltpu.VMEM((frames, span, channels), BF16),
            pltpu.VMEM((18, channels, channels), F32),
        ],
    )[0]


def sum_plane(packed, pieces):
    senders, taps, size, outs = packed.shape
    taps = taps - 1
    half = taps // 2

    def body(packed_ref, framed_ref, total):
        scales = [decoded_scale(packed_ref[s, taps])[:1, :1] for s in range(senders)]
        for tap in range(taps):
            acc = packed_ref[0, tap].astype(F32) * scales[0]
            for s in range(1, senders):
                acc += packed_ref[s, tap].astype(F32) * scales[s]
            total[tap] = acc
        place = 0
        for frame in range(2):
            for oct_ in range(size // 8):
                for lane in range(outs // 128):
                    piece = total[
                        frame * half : (frame + 1) * half,
                        oct_ * 8 : oct_ * 8 + 8,
                        lane * 128 : lane * 128 + 128,
                    ]
                    framed_ref[place] = framed(piece.reshape(half * 8, 128))
                    place += 1

    return pl.pallas_call(
        body,
        out_shape=jax.ShapeDtypeStruct((pieces, half * 8 + 8, 128), I16),
        scratch_shapes=[pltpu.VMEM((taps, size, outs), F32)],
        compiler_params=pltpu.CompilerParams(vmem_limit_bytes=VMEM_LIMIT),
    )(packed)


def sum_line(framed_parts, factor):
    def body(parts_ref, out_ref):
        acc = unframed(parts_ref[0])
        for s in range(1, framed_parts.shape[0]):
            acc += unframed(parts_ref[s])
        result = framed(acc * factor)
        for s in range(framed_parts.shape[0]):
            out_ref[s] = result

    return pl.pallas_call(
        body, out_shape=jax.ShapeDtypeStruct(framed_parts.shape, I16)
    )(framed_parts)


def unpack(plane, channels):
    parts, pieces, rows, _ = plane.shape
    size = channels // parts
    group = 4

    def body(plane_ref, out_ref):
        for part in range(group):
            place = 0
            for frame in range(2):
                for oct_ in range(size // 8):
                    for lane in range(channels // 128):
                        piece = unframed(plane_ref[part, place]).reshape(3, 3, 8, 128)
                        row = part * size + oct_ * 8
                        out_ref[frame, :, :, row : row + 8, lane * 128 : lane * 128 + 128] = piece
                        place += 1

    return pl.pallas_call(
        body,
        grid=(parts // group,),
        in_specs=[pl.BlockSpec((group, pieces, rows, 128), lambda k: (k, 0, 0, 0))],
        out_specs=pl.BlockSpec((2, 3, 3, group * size, channels), lambda k: (0, 0, 0, k, 0)),
        out_shape=jax.ShapeDtypeStruct((2, 3, 3, channels, channels), F32),
        compiler_params=pltpu.CompilerParams(vmem_limit_bytes=VMEM_LIMIT),
    )(plane)


def on_device(fields, kernels, codebook, codes):
    section_id = lax.axis_index("section")
    section = section_id.reshape(1).astype(jnp.int32)
    slab_id = lax.axis_index(SLAB)
    slabs = lax.axis_size(SLAB)
    own_field = fields[0]
    kernel = kernels[0]
    row_count, batch_count, frame_count, across, channels = own_field.shape
    book = codebook.shape[0]
    positions = row_count * batch_count * frame_count * across
    slots = max(16, 2 * positions // slabs)
    cells = (frame_count, row_count, batch_count * across, channels)

    edge = jnp.full((1,) + codes.shape[1:], -1, codes.dtype)
    shifted = jnp.concatenate([edge, codes, edge], axis=0)
    shifted = shifted.reshape(slabs + 1, row_count, batch_count, frame_count, across)
    shifted = jnp.transpose(shifted, (0, 3, 1, 2, 4)).reshape(slabs + 1, positions)
    wanted = lax.dynamic_slice_in_dim(shifted, section_id, slabs, 0)
    owner = jnp.where(wanted >= 0, wanted // book, -1)
    before = (
        lax.broadcasted_iota(jnp.int32, (positions, positions), 0)
        < lax.broadcasted_iota(jnp.int32, (positions, positions), 1)
    ).astype(BF16)

    mine = owner == slab_id
    rank = jnp.dot(mine.astype(BF16), before, preferred_element_type=F32).astype(jnp.int32)
    rank = jnp.where(mine, rank, -1)
    local = wanted - slab_id * book
    slot_ids = lax.broadcasted_iota(jnp.int32, (1, slots, 1), 1)
    asked = jnp.sum(jnp.where(rank[:, None, :] == slot_ids, local[:, None, :], 0), axis=-1)
    picks = (
        asked.reshape(-1, 1) == lax.broadcasted_iota(jnp.int32, (1, book), 1)
    ).astype(BF16)
    words = jnp.dot(picks, codebook, preferred_element_type=F32).astype(BF16)
    words = words.reshape(slabs, slots, channels)

    turned = own_field.reshape(row_count, batch_count, frame_count, slabs, row_count, channels)
    turned = jnp.transpose(turned, (3, 2, 4, 1, 0, 5)).reshape(slabs, -1, channels)
    arrived = exchange(jnp.concatenate([words, turned], axis=1), SLAB)
    looked = arrived[:, :slots].reshape(slabs * slots, channels)
    sent = lax.broadcasted_iota(jnp.int32, (positions, 1), 0)
    group, column = sent // across, sent % across
    sent = (column // row_count) * (positions // slabs) + group * row_count + column % row_count
    sent = (sent == lax.broadcasted_iota(jnp.int32, (1, positions), 1)).astype(BF16)
    cotangent = jnp.dot(
        sent, arrived[:, slots:].reshape(positions, channels), preferred_element_type=F32
    ).astype(BF16)
    cotangent = cotangent.reshape(frame_count, -1, channels)

    own_wanted = lax.dynamic_index_in_dim(wanted, slab_id, 0, keepdims=False)
    own_owner = lax.dynamic_index_in_dim(owner, slab_id, 0, keepdims=False)
    from_each = own_owner[None, :] == lax.broadcasted_iota(jnp.int32, (slabs, 1), 0)
    place = jnp.dot(from_each.astype(BF16), before, preferred_element_type=F32).astype(jnp.int32)
    place = jnp.sum(jnp.where(from_each, place, 0), axis=0)
    place = jnp.where(own_wanted >= 0, own_owner * slots + place, -1)
    gather = (
        place[:, None] == lax.broadcasted_iota(jnp.int32, (1, slabs * slots), 1)
    ).astype(BF16)
    fast = jnp.dot(gather, looked, preferred_element_type=F32).astype(BF16)

    every_owner = jnp.where(shifted >= 0, shifted // book, -1)[:, None, :]
    counts = jnp.sum(
        (every_owner == lax.broadcasted_iota(jnp.int32, (1, slabs, 1), 1)).astype(F32), axis=-1
    )
    crowded = jnp.full((lax.axis_size("dp"), 8, 128), jnp.max(counts) - slots)
    crowded = jnp.max(exchange(crowded, "dp")) > 0

    def whole_book(_):
        every = lax.all_gather(codebook, SLAB, axis=0, tiled=True)
        taken = jnp.take(every, jnp.maximum(own_wanted, 0), axis=0)
        return jnp.where(own_wanted[:, None] >= 0, taken, 0).astype(BF16)

    pair = lax.cond(crowded, whole_book, lambda quick: quick, fast)
    other = lax.ppermute(pair, "section", [(0, 1), (1, 0)])
    pair, other = pair.reshape(cells), other.reshape(cells)
    own = jnp.transpose(own_field, (2, 0, 1, 3, 4)).reshape(cells)
    above, below = neighbours(own[:, -1], own[:, 0])
    source = shift_source(section, pair, other, own, above, below, across)
    pre_act, dec_grad = convolve(section, source, kernel, cotangent)

    shaped = dec_grad.reshape(cells)
    above, below = neighbours(shaped[:, -1], shaped[:, 0])
    source = turn_source(section, source)
    back_dec = convolve_back(section, shaped, above, below, kernel, across)
    returned = lax.ppermute(back_dec, "section", [(1, 0)])

    total = (
        row_count * slabs * across * batch_count * lax.axis_size("dp") * frame_count
    )
    nx, ny, nz = lax.axis_size("x"), lax.axis_size("y"), lax.axis_size(Z)
    packed = kernel_grads(
        section, source, pre_act, dec_grad, returned, pair, other, nx * ny
    )
    plane = exchange(packed, ("y", "x"))
    line = exchange(sum_plane(plane, nz), Z)
    line = exchange(sum_line(line, 1.0 / math.sqrt(total)), Z)
    plane = exchange(jnp.broadcast_to(line[None], (nx * ny,) + line.shape), ("y", "x"))
    return unpack(plane, channels)[None]


def solution(mesh):
    sections, slabs, dps = (mesh.shape[a] for a in ("section", "slab", "dp"))
    nx = 4 if slabs >= 16 else 2
    inner = Mesh(
        mesh.devices.reshape(sections, slabs // (nx * nx), nx, nx, dps),
        ("section", "zh", "y", "x", "dp"),
    )
    placed = (
        P("section", SLAB, "dp", None, None, None),
        P("section", None, None, None, None, None),
        P(SLAB, None),
        P(None, "dp", None, None),
    )
    return jax.shard_map(
        on_device,
        mesh=inner,
        in_specs=placed,
        out_specs=P("section", None, None, None, None, None),
        check_vma=False,
    )
```

```python
import math

import jax
import jax.numpy as jnp
from jax import lax
from jax.experimental import pallas as pl
from jax.experimental.pallas import tpu as pltpu
from jax.sharding import Mesh, PartitionSpec as P

COMMIT = 0.5
SLAB = ("zh", "y", "x")
PLANE = ("y", "x")
Z = ("zh", "dp")
F32 = jnp.float32
BF16 = jnp.bfloat16
I16 = jnp.int16
TINY = 2.0**-100
STEPS = 32000.0
VMEM_LIMIT = 24 * 1024 * 1024


def silu_slope(pre_act):
    sig = jax.nn.sigmoid(pre_act)
    return sig * (1.0 + pre_act * (1.0 - sig))


def neighbours(lower, upper):
    count = lax.axis_size(SLAB)
    above = lax.ppermute(lower, SLAB, [(i, i + 1) for i in range(count - 1)])
    below = lax.ppermute(upper, SLAB, [(i + 1, i) for i in range(count - 1)])
    return above, below


def exchange(cells, axes):
    return lax.all_to_all(cells, axes, split_axis=0, concat_axis=0, tiled=True)


def coded(values):
    top = jnp.max(jnp.abs(values), axis=tuple(range(values.ndim)), keepdims=True)
    exponent = jnp.ceil(jnp.log2(top + TINY))
    return jnp.round(values * (jnp.exp2(-exponent) * STEPS)), exponent


def decoded_scale(exponents):
    return jnp.exp2(exponents.astype(F32)) * (1.0 / STEPS)


def framed(piece):
    steps, exponent = coded(piece)
    tail = jnp.broadcast_to(exponent, (8, 128))
    return jnp.concatenate([steps, tail], axis=0).astype(I16)


def unframed(rows):
    wide = rows.astype(F32)
    return wide[:-8] * (jnp.exp2(wide[-1:]) * (1.0 / STEPS))


def shifted_columns(block, across, tap):
    if tap == 1:
        return block
    count = block.shape[0]
    wide = block.astype(F32)
    column = lax.broadcasted_iota(jnp.int32, block.shape, 0) % across
    if tap == 0:
        wide = jnp.where(column == 0, 0.0, pltpu.roll(wide, 1, 0))
    else:
        wide = jnp.where(column == across - 1, 0.0, pltpu.roll(wide, count - 1, 0))
    return wide.astype(block.dtype)


def call(body, outs, *args, flops=0, scratch=()):
    size = sum(math.prod(a.shape) * a.dtype.itemsize for a in args) + sum(
        math.prod(o.shape) * o.dtype.itemsize for o in outs
    )
    return pl.pallas_call(
        body,
        in_specs=[pl.BlockSpec(memory_space=pltpu.SMEM)]
        + [pl.BlockSpec(memory_space=pltpu.VMEM)] * (len(args) - 1),
        out_specs=[pl.BlockSpec(memory_space=pltpu.VMEM)] * len(outs),
        out_shape=list(outs),
        scratch_shapes=list(scratch),
        cost_estimate=pl.CostEstimate(flops=flops, bytes_accessed=size, transcendentals=0),
        compiler_params=pltpu.CompilerParams(vmem_limit_bytes=VMEM_LIMIT),
    )(*args)


def shift_source(section, pair, other, own, above, below, across):
    frames, rows, count, channels = own.shape

    def body(section_ref, pair_ref, other_ref, own_ref, above_ref, below_ref, out_ref):
        def write(frame, row, block):
            for tap in range(3):
                out_ref[tap, frame, row] = shifted_columns(block, across, tap)

        @pl.when(section_ref[0] == 0)
        def _():
            for frame in range(frames):
                write(frame, 0, above_ref[frame])
                for row in range(rows):
                    write(frame, row + 1, own_ref[frame, row])
                write(frame, rows + 1, below_ref[frame])

        @pl.when(section_ref[0] == 1)
        def _():
            for frame in range(frames):
                for row in range(2):
                    write(frame, row, other_ref[frame, row])
                    write(frame, row + 2, pair_ref[frame, row])

    out = jax.ShapeDtypeStruct((3, frames, rows + 2, count, channels), BF16)
    return call(body, [out], section, pair, other, own, above, below)[0]


def turn_source(section, source):
    taps, frames, rows, count, channels = source.shape

    def body(section_ref, source_ref, out_ref):
        for tap in range(taps):
            for frame in range(frames):
                for row in range(rows):
                    start = (frame * rows + row) * count
                    out_ref[tap, :, start : start + count] = source_ref[tap, frame, row].T

    out = jax.ShapeDtypeStruct((taps, channels, frames * rows * count), BF16)
    return call(body, [out], section, source)[0]


def tap_index(section_ref, row_tap, column_tap):
    decoder = section_ref[0] == 1
    return jnp.where(decoder, column_tap, row_tap), jnp.where(decoder, row_tap, column_tap)


def convolve(section, source, kernel, cotangent):
    _, frames, rimmed, count, channels = source.shape
    rows = rimmed - 2
    span = rows * count

    def body(section_ref, source_ref, kernel_ref, cot_ref, pre_ref, grad_ref):
        for frame in range(frames):
            acc = jnp.zeros((span, channels), F32)
            for r in range(3):
                for q in range(3):
                    i, j = tap_index(section_ref, r, q)
                    for back in range(frame + 1):
                        cells = source_ref[q, frame - back, r : r + rows].reshape(span, channels)
                        acc += jnp.dot(
                            cells, kernel_ref[1 - back, i, j], preferred_element_type=F32
                        )
            pre_ref[frame] = acc
            grad_ref[frame] = (cot_ref[frame].astype(F32) * silu_slope(acc)).astype(BF16)

    shape = (frames, span, channels)
    return call(
        body,
        [jax.ShapeDtypeStruct(shape, F32), jax.ShapeDtypeStruct(shape, BF16)],
        section,
        source,
        kernel,
        cotangent,
        flops=54 * span * channels * channels,
    )


def convolve_back(section, grad, above, below, kernel, across):
    frames, rows, count, channels = grad.shape
    span = rows * count

    def body(section_ref, grad_ref, above_ref, below_ref, kernel_ref, out_ref, shifted):
        for frame in range(frames):
            blocks = [above_ref[frame]] + [grad_ref[frame, r] for r in range(rows)]
            for row, block in enumerate(blocks + [below_ref[frame]]):
                for tap in range(3):
                    shifted[tap, frame, row] = shifted_columns(block, across, tap)
        for frame in range(frames):
            acc = jnp.zeros((span, channels), F32)
            for r in range(3):
                for q in range(3):
                    i, j = tap_index(section_ref, r, q)
                    for ahead in range(frames - frame):
                        cells = shifted[2 - q, frame + ahead, 2 - r : 2 - r + rows]
                        acc += lax.dot_general(
                            cells.reshape(span, channels),
                            kernel_ref[1 - ahead, i, j],
                            (((1,), (1,)), ((), ())),
                            preferred_element_type=F32,
                        )
            out_ref[frame] = acc.astype(BF16).reshape(rows, count, channels)

    return call(
        body,
        [jax.ShapeDtypeStruct(grad.shape, BF16)],
        section,
        grad,
        above,
        below,
        kernel,
        flops=54 * span * channels * channels,
        scratch=[pltpu.VMEM((3, frames, rows + 2, count, channels), BF16)],
    )[0]


def kernel_grads(section, turned, pre_act, dec_grad, returned, pair, other, parts):
    _, channels, _ = turned.shape
    frames, rows, count, _ = returned.shape
    span = rows * count
    size = channels // parts

    def body(
        section_ref, turned_ref, pre_ref, dec_ref, returned_ref, pair_ref, other_ref,
        out_ref, side, grads,
    ):
        @pl.when(section_ref[0] == 0)
        def _():
            for frame in range(frames):
                for row, quant in enumerate((pair_ref[frame, 1], other_ref[frame, 0])):
                    at = slice(row * count, (row + 1) * count)
                    side[frame, at] = (
                        returned_ref[frame, row].astype(F32)
                        + COMMIT * (pre_ref[frame, at] - quant.astype(F32))
                    ).astype(BF16)

        @pl.when(section_ref[0] == 1)
        def _():
            side[...] = dec_ref[...]

        top = jnp.zeros((8, channels), F32)
        for r in range(3):
            for q in range(3):
                i, j = tap_index(section_ref, r, q)
                tap = i * 3 + j
                first = turned_ref[q, :, r * count : r * count + span]
                start = (rows + 2 + r) * count
                second = turned_ref[q, :, start : start + span]
                late = jnp.dot(first, side[1], preferred_element_type=F32)
                same = jnp.dot(first, side[0], preferred_element_type=F32)
                same += jnp.dot(second, side[1], preferred_element_type=F32)
                for at, values in ((tap, late), (9 + tap, same)):
                    grads[at] = values
                    seen = jnp.max(jnp.abs(values).reshape(-1, 8, channels), axis=0)
                    top = jnp.maximum(top, seen)
        exponent = jnp.ceil(jnp.log2(jnp.max(top, axis=(0, 1), keepdims=True) + TINY))
        factor = jnp.exp2(-exponent) * STEPS

        @pl.loop(0, 18)
        def _(tap):
            steps = jnp.round(grads[tap] * factor).astype(I16)
            out_ref[:, tap] = steps.reshape(parts, size, channels)

        tail = jnp.broadcast_to(exponent, (size, channels)).astype(I16)
        for part in range(parts):
            out_ref[part, 18] = tail

    return call(
        body,
        [jax.ShapeDtypeStruct((parts, 19, size, channels), I16)],
        section,
        turned,
        pre_act,
        dec_grad,
        returned,
        pair,
        other,
        flops=54 * span * channels * channels,
        scratch=[
            pltpu.VMEM((frames, span, channels), BF16),
            pltpu.VMEM((18, channels, channels), F32),
        ],
    )[0]


def sum_plane(packed, pieces):
    senders, taps, size, outs = packed.shape
    taps = taps - 1
    half = taps // 2

    def body(packed_ref, framed_ref, total):
        scales = [decoded_scale(packed_ref[s, taps])[:1, :1] for s in range(senders)]
        for tap in range(taps):
            acc = packed_ref[0, tap].astype(F32) * scales[0]
            for s in range(1, senders):
                acc += packed_ref[s, tap].astype(F32) * scales[s]
            total[tap] = acc
        place = 0
        for frame in range(2):
            for oct_ in range(size // 8):
                for lane in range(outs // 128):
                    piece = total[
                        frame * half : (frame + 1) * half,
                        oct_ * 8 : oct_ * 8 + 8,
                        lane * 128 : lane * 128 + 128,
                    ]
                    framed_ref[place] = framed(piece.reshape(half * 8, 128))
                    place += 1

    return pl.pallas_call(
        body,
        out_shape=jax.ShapeDtypeStruct((pieces, half * 8 + 8, 128), I16),
        scratch_shapes=[pltpu.VMEM((taps, size, outs), F32)],
        compiler_params=pltpu.CompilerParams(vmem_limit_bytes=VMEM_LIMIT),
    )(packed)


def sum_line(framed_parts, factor):
    def body(parts_ref, out_ref):
        acc = unframed(parts_ref[0])
        for s in range(1, framed_parts.shape[0]):
            acc += unframed(parts_ref[s])
        result = framed(acc * factor)
        for s in range(framed_parts.shape[0]):
            out_ref[s] = result

    return pl.pallas_call(
        body, out_shape=jax.ShapeDtypeStruct(framed_parts.shape, I16)
    )(framed_parts)


def unpack(plane, channels):
    parts, pieces, rows, _ = plane.shape
    size = channels // parts
    group = 4

    def body(plane_ref, out_ref):
        for part in range(group):
            place = 0
            for frame in range(2):
                for oct_ in range(size // 8):
                    for lane in range(channels // 128):
                        piece = unframed(plane_ref[part, place]).reshape(3, 3, 8, 128)
                        row = part * size + oct_ * 8
                        out_ref[frame, :, :, row : row + 8, lane * 128 : lane * 128 + 128] = piece
                        place += 1

    return pl.pallas_call(
        body,
        grid=(parts // group,),
        in_specs=[pl.BlockSpec((group, pieces, rows, 128), lambda k: (k, 0, 0, 0))],
        out_specs=pl.BlockSpec((2, 3, 3, group * size, channels), lambda k: (0, 0, 0, k, 0)),
        out_shape=jax.ShapeDtypeStruct((2, 3, 3, channels, channels), F32),
        compiler_params=pltpu.CompilerParams(vmem_limit_bytes=VMEM_LIMIT),
    )(plane)


def front(own_field, codebook, codes):
    section_id = lax.axis_index("section")
    slab_id = lax.axis_index(SLAB)
    slabs = lax.axis_size(SLAB)
    near = lax.axis_index("zh")
    plane_id = lax.axis_index(PLANE)
    planes = lax.axis_size(PLANE)
    halves = slabs // planes
    row_count, batch_count, frame_count, across, channels = own_field.shape
    book = codebook.shape[0]
    positions = row_count * batch_count * frame_count * across
    mean = positions // planes
    slots = int(mean + 6 * math.sqrt(mean) + 15) // 16 * 16
    cells = (frame_count, row_count, batch_count * across, channels)

    half = book // 2
    got = lax.ppermute(
        lax.dynamic_slice_in_dim(codebook, section_id * half, half, 0), "zh", [(0, 1), (1, 0)]
    )
    table = jnp.concatenate(
        [codebook, got, lax.ppermute(got, "section", [(0, 1), (1, 0)])], axis=0
    )

    turned = own_field.reshape(
        row_count, batch_count, frame_count, halves, planes, row_count, channels
    )
    turned = jnp.transpose(turned, (3, 4, 2, 5, 1, 0, 6)).reshape(halves, planes, -1, channels)
    kept = lax.dynamic_index_in_dim(turned, near, 0, keepdims=False)
    passed = lax.dynamic_index_in_dim(turned, 1 - near, 0, keepdims=False)
    passed = lax.ppermute(passed, ("section", "zh"), [(2, 3), (3, 2)])

    own = jnp.transpose(own_field, (2, 0, 1, 3, 4)).reshape(cells)
    above, below = neighbours(own[:, -1], own[:, 0])

    edge = jnp.full((1,) + codes.shape[1:], -1, codes.dtype)
    shifted = jnp.concatenate([edge, codes, edge], axis=0)
    shifted = shifted.reshape(slabs + 1, row_count, batch_count, frame_count, across)
    shifted = jnp.transpose(shifted, (0, 3, 1, 2, 4)).reshape(slabs + 1, positions)
    holder = jnp.where(shifted >= 0, shifted // book % planes, -1)

    counts = jnp.sum(
        (holder[:, None, :] == lax.broadcasted_iota(jnp.int32, (1, planes, 1), 1)).astype(F32), axis=-1
    )
    crowded = jnp.full((lax.axis_size("dp"), 8, 128), jnp.max(counts) - slots)
    crowded = exchange(crowded, "dp")

    before = (
        lax.broadcasted_iota(jnp.int32, (positions, positions), 0)
        < lax.broadcasted_iota(jnp.int32, (positions, positions), 1)
    ).astype(BF16)

    start = near * planes + section_id
    wanted = lax.dynamic_slice_in_dim(shifted, start, planes, 0)
    mine = lax.dynamic_slice_in_dim(holder, start, planes, 0) == plane_id
    rank = jnp.dot(mine.astype(BF16), before, preferred_element_type=F32).astype(jnp.int32)
    rank = jnp.where(mine, rank, -1)
    within = wanted % book
    far = book + jnp.where(within // half == section_id, 0, half) + within % half
    local = jnp.where(wanted // book == slab_id, within, far)
    slot_ids = lax.broadcasted_iota(jnp.int32, (1, slots, 1), 1)
    asked = jnp.sum(jnp.where(rank[:, None, :] == slot_ids, local[:, None, :], 0), axis=-1)
    picks = (
        asked.reshape(-1, 1) == lax.broadcasted_iota(jnp.int32, (1, 2 * book), 1)
    ).astype(BF16)
    table, passed, above, below, crowded = lax.optimization_barrier(
        (table, passed, above, below, crowded)
    )
    words = jnp.dot(picks, table, preferred_element_type=F32).astype(BF16)
    words = words.reshape(planes, slots, channels)

    arrived = exchange(jnp.concatenate([words, kept, passed], axis=1), PLANE)
    looked = arrived[:, :slots].reshape(planes * slots, channels)

    place = lax.broadcasted_iota(jnp.int32, (positions, 1), 0)
    group, column = place // across, place % across
    source = column // row_count
    share = positions // slabs
    place = (source % planes) * (halves * share) + jnp.where(source // planes == near, 0, share)
    place = place + group * row_count + column % row_count
    sent = (place == lax.broadcasted_iota(jnp.int32, (1, positions), 1)).astype(BF16)
    cotangent = jnp.dot(
        sent, arrived[:, slots:].reshape(positions, channels), preferred_element_type=F32
    ).astype(BF16)

    own_wanted = lax.dynamic_index_in_dim(shifted, slab_id + section_id, 0, keepdims=False)
    own_holder = lax.dynamic_index_in_dim(holder, slab_id + section_id, 0, keepdims=False)
    from_each = own_holder[None, :] == lax.broadcasted_iota(jnp.int32, (planes, 1), 0)
    order = jnp.dot(from_each.astype(BF16), before, preferred_element_type=F32).astype(jnp.int32)
    order = jnp.sum(jnp.where(from_each, order, 0), axis=0)
    order = jnp.where(own_wanted >= 0, own_holder * slots + order, -1)
    gather = (
        order[:, None] == lax.broadcasted_iota(jnp.int32, (1, planes * slots), 1)
    ).astype(BF16)
    fast = jnp.dot(gather, looked, preferred_element_type=F32).astype(BF16)

    def whole_book(_):
        every = lax.all_gather(codebook, SLAB, axis=0, tiled=True)
        taken = jnp.take(every, jnp.maximum(own_wanted, 0), axis=0)
        return jnp.where(own_wanted[:, None] >= 0, taken, 0).astype(BF16)

    pair = lax.cond(jnp.max(crowded) > 0, whole_book, lambda quick: quick, fast)
    other = lax.ppermute(pair, "section", [(0, 1), (1, 0)])
    return (
        pair.reshape(cells),
        other.reshape(cells),
        cotangent.reshape(frame_count, -1, channels),
        own,
        above,
        below,
    )


def on_device(fields, kernels, codebook, codes):
    section = lax.axis_index("section").reshape(1).astype(jnp.int32)
    slabs = lax.axis_size(SLAB)
    own_field = fields[0]
    kernel = kernels[0]
    row_count, batch_count, frame_count, across, channels = own_field.shape
    cells = (frame_count, row_count, batch_count * across, channels)
    pair, other, cotangent, own, above, below = front(own_field, codebook, codes)
    source = shift_source(section, pair, other, own, above, below, across)
    pre_act, dec_grad = convolve(section, source, kernel, cotangent)

    shaped = dec_grad.reshape(cells)
    above, below = neighbours(shaped[:, -1], shaped[:, 0])
    source = turn_source(section, source)
    back_dec = convolve_back(section, shaped, above, below, kernel, across)
    returned = lax.ppermute(back_dec, "section", [(1, 0)])

    total = (
        row_count * slabs * across * batch_count * lax.axis_size("dp") * frame_count
    )
    nx, ny, nz = lax.axis_size("x"), lax.axis_size("y"), lax.axis_size(Z)
    packed = kernel_grads(
        section, source, pre_act, dec_grad, returned, pair, other, nx * ny
    )
    plane = exchange(packed, PLANE)
    line = exchange(sum_plane(plane, nz), Z)
    line = exchange(sum_line(line, 1.0 / math.sqrt(total)), Z)
    plane = exchange(jnp.broadcast_to(line[None], (nx * ny,) + line.shape), PLANE)
    return unpack(plane, channels)[None]


def solution(mesh):
    sections, slabs, dps = (mesh.shape[a] for a in ("section", "slab", "dp"))
    nx = 4 if slabs >= 16 else 2
    inner = Mesh(
        mesh.devices.reshape(sections, slabs // (nx * nx), nx, nx, dps),
        ("section", "zh", "y", "x", "dp"),
    )
    placed = (
        P("section", SLAB, "dp", None, None, None),
        P("section", None, None, None, None, None),
        P(SLAB, None),
        P(None, "dp", None, None),
    )
    return jax.shard_map(
        on_device,
        mesh=inner,
        in_specs=placed,
        out_specs=P("section", None, None, None, None, None),
        check_vma=False,
    )
```

```python
import math

import jax
import jax.numpy as jnp
from jax import lax
from jax.experimental import pallas as pl
from jax.experimental.pallas import tpu as pltpu
from jax.sharding import Mesh, PartitionSpec as P

COMMIT = 0.5
SLAB = ("zh", "y", "x")
PLANE = ("y", "x")
Z = ("zh", "dp")
F32 = jnp.float32
BF16 = jnp.bfloat16
I16 = jnp.int16
TINY = 2.0**-100
STEPS = 32000.0
VMEM_LIMIT = 24 * 1024 * 1024


def silu_slope(pre_act):
    sig = jax.nn.sigmoid(pre_act)
    return sig * (1.0 + pre_act * (1.0 - sig))


def neighbours(lower, upper):
    count = lax.axis_size(SLAB)
    above = lax.ppermute(lower, SLAB, [(i, i + 1) for i in range(count - 1)])
    below = lax.ppermute(upper, SLAB, [(i + 1, i) for i in range(count - 1)])
    return above, below


def exchange(cells, axes):
    return lax.all_to_all(cells, axes, split_axis=0, concat_axis=0, tiled=True)


def coded(values):
    top = jnp.max(jnp.abs(values), axis=tuple(range(values.ndim)), keepdims=True)
    exponent = jnp.ceil(jnp.log2(top + TINY))
    return jnp.round(values * (jnp.exp2(-exponent) * STEPS)), exponent


def decoded_scale(exponents):
    return jnp.exp2(exponents.astype(F32)) * (1.0 / STEPS)


def framed(piece, mark):
    steps, exponent = coded(piece)
    row = lax.broadcasted_iota(jnp.int32, (8, 128), 0)
    tail = jnp.where(row == 0, mark, exponent)
    return jnp.concatenate([steps, tail], axis=0).astype(I16)


def unframed(wide):
    return wide[:-8] * (jnp.exp2(wide[-1:]) * (1.0 / STEPS))


def shifted_columns(block, across, tap):
    if tap == 1:
        return block
    count = block.shape[0]
    wide = block.astype(F32)
    column = lax.broadcasted_iota(jnp.int32, block.shape, 0) % across
    if tap == 0:
        wide = jnp.where(column == 0, 0.0, pltpu.roll(wide, 1, 0))
    else:
        wide = jnp.where(column == across - 1, 0.0, pltpu.roll(wide, count - 1, 0))
    return wide.astype(block.dtype)


def call(body, outs, *args, flops=0, scratch=()):
    size = sum(math.prod(a.shape) * a.dtype.itemsize for a in args) + sum(
        math.prod(o.shape) * o.dtype.itemsize for o in outs
    )
    return pl.pallas_call(
        body,
        in_specs=[pl.BlockSpec(memory_space=pltpu.SMEM)]
        + [pl.BlockSpec(memory_space=pltpu.VMEM)] * (len(args) - 1),
        out_specs=[pl.BlockSpec(memory_space=pltpu.VMEM)] * len(outs),
        out_shape=list(outs),
        scratch_shapes=list(scratch),
        cost_estimate=pl.CostEstimate(flops=flops, bytes_accessed=size, transcendentals=0),
        compiler_params=pltpu.CompilerParams(vmem_limit_bytes=VMEM_LIMIT),
    )(*args)


def shift_source(section, pair, other, own, above, below, across):
    frames, rows, count, channels = own.shape

    def body(section_ref, pair_ref, other_ref, own_ref, above_ref, below_ref, out_ref):
        def write(frame, row, block):
            for tap in range(3):
                out_ref[tap, frame, row] = shifted_columns(block, across, tap)

        @pl.when(section_ref[0] == 0)
        def _():
            for frame in range(frames):
                write(frame, 0, above_ref[frame])
                for row in range(rows):
                    write(frame, row + 1, own_ref[frame, row])
                write(frame, rows + 1, below_ref[frame])

        @pl.when(section_ref[0] == 1)
        def _():
            for frame in range(frames):
                for row in range(2):
                    write(frame, row, other_ref[frame, row])
                    write(frame, row + 2, pair_ref[frame, row])

    out = jax.ShapeDtypeStruct((3, frames, rows + 2, count, channels), BF16)
    return call(body, [out], section, pair, other, own, above, below)[0]


def turn_source(section, source):
    taps, frames, rows, count, channels = source.shape

    def body(section_ref, source_ref, out_ref):
        for tap in range(taps):
            for frame in range(frames):
                for row in range(rows):
                    start = (frame * rows + row) * count
                    out_ref[tap, :, start : start + count] = source_ref[tap, frame, row].T

    out = jax.ShapeDtypeStruct((taps, channels, frames * rows * count), BF16)
    return call(body, [out], section, source)[0]


def tap_index(section_ref, row_tap, column_tap):
    decoder = section_ref[0] == 1
    return jnp.where(decoder, column_tap, row_tap), jnp.where(decoder, row_tap, column_tap)


def convolve(section, source, kernel, cotangent):
    _, frames, rimmed, count, channels = source.shape
    rows = rimmed - 2
    span = rows * count

    def body(section_ref, source_ref, kernel_ref, cot_ref, pre_ref, grad_ref):
        for frame in range(frames):
            acc = jnp.zeros((span, channels), F32)
            for r in range(3):
                for q in range(3):
                    i, j = tap_index(section_ref, r, q)
                    for back in range(frame + 1):
                        cells = source_ref[q, frame - back, r : r + rows].reshape(span, channels)
                        acc += jnp.dot(
                            cells, kernel_ref[1 - back, i, j], preferred_element_type=F32
                        )
            pre_ref[frame] = acc
            grad_ref[frame] = (cot_ref[frame].astype(F32) * silu_slope(acc)).astype(BF16)

    shape = (frames, span, channels)
    return call(
        body,
        [jax.ShapeDtypeStruct(shape, F32), jax.ShapeDtypeStruct(shape, BF16)],
        section,
        source,
        kernel,
        cotangent,
        flops=54 * span * channels * channels,
    )


def convolve_back(section, grad, above, below, kernel, across):
    frames, rows, count, channels = grad.shape
    span = rows * count

    def body(section_ref, grad_ref, above_ref, below_ref, kernel_ref, out_ref, shifted):
        for frame in range(frames):
            blocks = [above_ref[frame]] + [grad_ref[frame, r] for r in range(rows)]
            for row, block in enumerate(blocks + [below_ref[frame]]):
                for tap in range(3):
                    shifted[tap, frame, row] = shifted_columns(block, across, tap)
        for frame in range(frames):
            acc = jnp.zeros((span, channels), F32)
            for r in range(3):
                for q in range(3):
                    i, j = tap_index(section_ref, r, q)
                    for ahead in range(frames - frame):
                        cells = shifted[2 - q, frame + ahead, 2 - r : 2 - r + rows]
                        acc += lax.dot_general(
                            cells.reshape(span, channels),
                            kernel_ref[1 - ahead, i, j],
                            (((1,), (1,)), ((), ())),
                            preferred_element_type=F32,
                        )
            out_ref[frame] = acc.astype(BF16).reshape(rows, count, channels)

    return call(
        body,
        [jax.ShapeDtypeStruct(grad.shape, BF16)],
        section,
        grad,
        above,
        below,
        kernel,
        flops=54 * span * channels * channels,
        scratch=[pltpu.VMEM((3, frames, rows + 2, count, channels), BF16)],
    )[0]


def kernel_grads(section, turned, pre_act, dec_grad, returned, pair, other, parts):
    _, channels, _ = turned.shape
    frames, rows, count, _ = returned.shape
    span = rows * count
    size = channels // parts

    def body(
        section_ref, turned_ref, pre_ref, dec_ref, returned_ref, pair_ref, other_ref,
        out_ref, side, grads,
    ):
        @pl.when(section_ref[0] == 0)
        def _():
            for frame in range(frames):
                for row, quant in enumerate((pair_ref[frame, 1], other_ref[frame, 0])):
                    at = slice(row * count, (row + 1) * count)
                    side[frame, at] = (
                        returned_ref[frame, row].astype(F32)
                        + COMMIT * (pre_ref[frame, at] - quant.astype(F32))
                    ).astype(BF16)

        @pl.when(section_ref[0] == 1)
        def _():
            side[...] = dec_ref[...]

        top = jnp.zeros((8, channels), F32)
        for r in range(3):
            for q in range(3):
                i, j = tap_index(section_ref, r, q)
                tap = i * 3 + j
                first = turned_ref[q, :, r * count : r * count + span]
                start = (rows + 2 + r) * count
                second = turned_ref[q, :, start : start + span]
                late = jnp.dot(first, side[1], preferred_element_type=F32)
                same = jnp.dot(first, side[0], preferred_element_type=F32)
                same += jnp.dot(second, side[1], preferred_element_type=F32)
                for at, values in ((tap, late), (9 + tap, same)):
                    grads[at] = values
                    seen = jnp.max(jnp.abs(values).reshape(-1, 8, channels), axis=0)
                    top = jnp.maximum(top, seen)
        exponent = jnp.ceil(jnp.log2(jnp.max(top, axis=(0, 1), keepdims=True) + TINY))
        factor = jnp.exp2(-exponent) * STEPS

        @pl.loop(0, 18)
        def _(tap):
            steps = jnp.round(grads[tap] * factor).astype(I16)
            out_ref[:, tap] = steps.reshape(parts, size, channels)

        tail = jnp.broadcast_to(exponent, (size, channels)).astype(I16)
        for part in range(parts):
            out_ref[part, 18] = tail

    return call(
        body,
        [jax.ShapeDtypeStruct((parts, 19, size, channels), I16)],
        section,
        turned,
        pre_act,
        dec_grad,
        returned,
        pair,
        other,
        flops=54 * span * channels * channels,
        scratch=[
            pltpu.VMEM((frames, span, channels), BF16),
            pltpu.VMEM((18, channels, channels), F32),
        ],
    )[0]


def sum_plane(crowded, packed, pieces):
    senders, taps, size, outs = packed.shape
    taps = taps - 1
    half = taps // 2

    def body(crowded_ref, packed_ref, framed_ref, total):
        mark = jnp.full((1, 128), crowded_ref[0])
        scales = [decoded_scale(packed_ref[s, taps])[:1, :1] for s in range(senders)]
        for tap in range(taps):
            acc = packed_ref[0, tap].astype(F32) * scales[0]
            for s in range(1, senders):
                acc += packed_ref[s, tap].astype(F32) * scales[s]
            total[tap] = acc
        place = 0
        for frame in range(2):
            for oct_ in range(size // 8):
                for lane in range(outs // 128):
                    piece = total[
                        frame * half : (frame + 1) * half,
                        oct_ * 8 : oct_ * 8 + 8,
                        lane * 128 : lane * 128 + 128,
                    ]
                    framed_ref[place] = framed(piece.reshape(half * 8, 128), mark)
                    place += 1

    return pl.pallas_call(
        body,
        in_specs=[
            pl.BlockSpec(memory_space=pltpu.SMEM),
            pl.BlockSpec(memory_space=pltpu.VMEM),
        ],
        out_shape=jax.ShapeDtypeStruct((pieces, half * 8 + 8, 128), I16),
        scratch_shapes=[pltpu.VMEM((taps, size, outs), F32)],
        compiler_params=pltpu.CompilerParams(vmem_limit_bytes=VMEM_LIMIT),
    )(crowded, packed)


def sum_line(framed_parts, factor):
    def body(parts_ref, out_ref):
        first = parts_ref[0].astype(F32)
        acc, mark = unframed(first), first[-8:-7]
        for s in range(1, framed_parts.shape[0]):
            part = parts_ref[s].astype(F32)
            acc += unframed(part)
            mark = jnp.maximum(mark, part[-8:-7])
        result = framed(acc * factor, mark)
        for s in range(framed_parts.shape[0]):
            out_ref[s] = result

    return pl.pallas_call(
        body, out_shape=jax.ShapeDtypeStruct(framed_parts.shape, I16)
    )(framed_parts)


def unpack(plane, channels):
    parts, pieces, rows, _ = plane.shape
    size = channels // parts
    group = 4

    def body(plane_ref, out_ref):
        for part in range(group):
            place = 0
            for frame in range(2):
                for oct_ in range(size // 8):
                    for lane in range(channels // 128):
                        piece = unframed(plane_ref[part, place].astype(F32)).reshape(3, 3, 8, 128)
                        row = part * size + oct_ * 8
                        out_ref[frame, :, :, row : row + 8, lane * 128 : lane * 128 + 128] = piece
                        place += 1

    return pl.pallas_call(
        body,
        grid=(parts // group,),
        in_specs=[pl.BlockSpec((group, pieces, rows, 128), lambda k: (k, 0, 0, 0))],
        out_specs=pl.BlockSpec((2, 3, 3, group * size, channels), lambda k: (0, 0, 0, k, 0)),
        out_shape=jax.ShapeDtypeStruct((2, 3, 3, channels, channels), F32),
        compiler_params=pltpu.CompilerParams(vmem_limit_bytes=VMEM_LIMIT),
    )(plane)


def routed(codebook, shifted, holder, slots, turned, above, below):
    section_id = lax.axis_index("section")
    slab_id = lax.axis_index(SLAB)
    near = lax.axis_index("zh")
    plane_id = lax.axis_index(PLANE)
    planes = lax.axis_size(PLANE)
    book, channels = codebook.shape
    positions = shifted.shape[1]

    half = book // 2
    got = lax.ppermute(
        lax.dynamic_slice_in_dim(codebook, section_id * half, half, 0), "zh", [(0, 1), (1, 0)]
    )
    table = jnp.concatenate(
        [codebook, got, lax.ppermute(got, "section", [(0, 1), (1, 0)])], axis=0
    )

    before = (
        lax.broadcasted_iota(jnp.int32, (positions, positions), 0)
        < lax.broadcasted_iota(jnp.int32, (positions, positions), 1)
    ).astype(BF16)

    start = near * planes + section_id
    wanted = lax.dynamic_slice_in_dim(shifted, start, planes, 0)
    mine = lax.dynamic_slice_in_dim(holder, start, planes, 0) == plane_id
    rank = jnp.dot(mine.astype(BF16), before, preferred_element_type=F32).astype(jnp.int32)
    rank = jnp.where(mine, rank, -1)
    within = wanted % book
    far = book + jnp.where(within // half == section_id, 0, half) + within % half
    local = jnp.where(wanted // book == slab_id, within, far)
    slot_ids = lax.broadcasted_iota(jnp.int32, (1, slots, 1), 1)
    asked = jnp.sum(jnp.where(rank[:, None, :] == slot_ids, local[:, None, :], 0), axis=-1)
    picks = (
        asked.reshape(-1, 1) == lax.broadcasted_iota(jnp.int32, (1, 2 * book), 1)
    ).astype(BF16)
    table, turned = lax.optimization_barrier((table, turned))
    words = jnp.dot(picks, table, preferred_element_type=F32).astype(BF16)
    looked = exchange(words.reshape(planes, slots, channels), PLANE)
    looked = looked.reshape(planes * slots, channels)
    looked, above, below = lax.optimization_barrier((looked, above, below))

    own_wanted = lax.dynamic_index_in_dim(shifted, slab_id + section_id, 0, keepdims=False)
    own_holder = lax.dynamic_index_in_dim(holder, slab_id + section_id, 0, keepdims=False)
    from_each = own_holder[None, :] == lax.broadcasted_iota(jnp.int32, (planes, 1), 0)
    order = jnp.dot(from_each.astype(BF16), before, preferred_element_type=F32).astype(jnp.int32)
    order = jnp.sum(jnp.where(from_each, order, 0), axis=0)
    order = jnp.where(own_wanted >= 0, own_holder * slots + order, -1)
    gather = (
        order[:, None] == lax.broadcasted_iota(jnp.int32, (1, planes * slots), 1)
    ).astype(BF16)
    pair = jnp.dot(gather, looked, preferred_element_type=F32).astype(BF16)
    return pair, turned, above, below


def front(own_field, codebook, codes, whole):
    section_id = lax.axis_index("section")
    slab_id = lax.axis_index(SLAB)
    slabs = lax.axis_size(SLAB)
    planes = lax.axis_size(PLANE)
    row_count, batch_count, frame_count, across, channels = own_field.shape
    book = codebook.shape[0]
    positions = row_count * batch_count * frame_count * across
    mean = positions // planes
    slots = int(mean + 6 * math.sqrt(mean) + 15) // 16 * 16
    cells = (frame_count, row_count, batch_count * across, channels)

    turned = own_field.reshape(row_count, batch_count, frame_count, slabs, row_count, channels)
    turned = jnp.transpose(turned, (3, 2, 4, 1, 0, 5)).reshape(slabs, -1, channels)
    turned = exchange(turned, SLAB).reshape(positions, channels)

    own = jnp.transpose(own_field, (2, 0, 1, 3, 4)).reshape(cells)
    above, below = neighbours(own[:, -1], own[:, 0])

    edge = jnp.full((1,) + codes.shape[1:], -1, codes.dtype)
    shifted = jnp.concatenate([edge, codes, edge], axis=0)
    shifted = shifted.reshape(slabs + 1, row_count, batch_count, frame_count, across)
    shifted = jnp.transpose(shifted, (0, 3, 1, 2, 4)).reshape(slabs + 1, positions)
    holder = jnp.where(shifted >= 0, shifted // book % planes, -1)

    if whole:
        wanted = lax.dynamic_index_in_dim(shifted, slab_id + section_id, 0, keepdims=False)
        every = lax.all_gather(codebook, SLAB, axis=0, tiled=True)
        taken = jnp.take(every, jnp.maximum(wanted, 0), axis=0)
        pair = jnp.where(wanted[:, None] >= 0, taken, 0).astype(BF16)
    else:
        pair, turned, above, below = routed(
            codebook, shifted, holder, slots, turned, above, below
        )

    place = lax.broadcasted_iota(jnp.int32, (positions, 1), 0)
    group, column = place // across, place % across
    place = (column // row_count) * (positions // slabs) + group * row_count + column % row_count
    sent = (place == lax.broadcasted_iota(jnp.int32, (1, positions), 1)).astype(BF16)
    cotangent = jnp.dot(sent, turned, preferred_element_type=F32).astype(BF16)

    counts = jnp.sum(
        (holder[:, None, :] == lax.broadcasted_iota(jnp.int32, (1, planes, 1), 1)).astype(F32), axis=-1
    )
    crowded = (jnp.max(counts) > slots).astype(F32).reshape(1)

    other = lax.ppermute(pair, "section", [(0, 1), (1, 0)])
    return (
        pair.reshape(cells),
        other.reshape(cells),
        cotangent.reshape(frame_count, -1, channels),
        own,
        above,
        below,
        crowded,
    )


def line_shares(fields, kernels, codebook, codes, whole):
    section = lax.axis_index("section").reshape(1).astype(jnp.int32)
    slabs = lax.axis_size(SLAB)
    own_field = fields[0]
    kernel = kernels[0]
    row_count, batch_count, frame_count, across, channels = own_field.shape
    cells = (frame_count, row_count, batch_count * across, channels)
    pair, other, cotangent, own, above, below, crowded = front(own_field, codebook, codes, whole)
    source = shift_source(section, pair, other, own, above, below, across)
    pre_act, dec_grad = convolve(section, source, kernel, cotangent)

    shaped = dec_grad.reshape(cells)
    above, below = neighbours(shaped[:, -1], shaped[:, 0])
    source = turn_source(section, source)
    back_dec = convolve_back(section, shaped, above, below, kernel, across)
    returned = lax.ppermute(back_dec, "section", [(1, 0)])

    total = (
        row_count * slabs * across * batch_count * lax.axis_size("dp") * frame_count
    )
    packed = kernel_grads(
        section, source, pre_act, dec_grad, returned, pair, other, lax.axis_size(PLANE)
    )
    plane = exchange(packed, PLANE)
    line = exchange(sum_plane(crowded, plane, lax.axis_size(Z)), Z)
    return exchange(sum_line(line, 1.0 / math.sqrt(total)), Z)


def on_device(fields, kernels, codebook, codes):
    line = line_shares(fields, kernels, codebook, codes, False)
    line = lax.cond(
        jnp.max(line[:, -8]) > 0,
        lambda frames, *args: line_shares(*args, True),
        lambda frames, *args: frames,
        line,
        fields,
        kernels,
        codebook,
        codes,
    )
    planes = lax.axis_size(PLANE)
    plane = exchange(jnp.broadcast_to(line[None], (planes,) + line.shape), PLANE)
    return unpack(plane, kernels.shape[-1])[None]


def solution(mesh):
    sections, slabs, dps = (mesh.shape[a] for a in ("section", "slab", "dp"))
    nx = 4 if slabs >= 16 else 2
    inner = Mesh(
        mesh.devices.reshape(sections, slabs // (nx * nx), nx, nx, dps),
        ("section", "zh", "y", "x", "dp"),
    )
    placed = (
        P("section", SLAB, "dp", None, None, None),
        P("section", None, None, None, None, None),
        P(SLAB, None),
        P(None, "dp", None, None),
    )
    return jax.shard_map(
        on_device,
        mesh=inner,
        in_specs=placed,
        out_specs=P("section", None, None, None, None, None),
        check_vma=False,
    )
```

```python
import math

import jax
import jax.numpy as jnp
from jax import lax
from jax.experimental import pallas as pl
from jax.experimental.pallas import tpu as pltpu
from jax.sharding import Mesh, PartitionSpec as P

COMMIT = 0.5
SLAB = ("zh", "y", "x")
PLANE = ("y", "x")
Z = ("zh", "dp")
F32 = jnp.float32
BF16 = jnp.bfloat16
I16 = jnp.int16
TINY = 2.0**-100
STEPS = 32000.0
VMEM_LIMIT = 24 * 1024 * 1024


def silu_slope(pre_act):
    sig = jax.nn.sigmoid(pre_act)
    return sig * (1.0 + pre_act * (1.0 - sig))


def neighbours(lower, upper):
    count = lax.axis_size(SLAB)
    above = lax.ppermute(lower, SLAB, [(i, i + 1) for i in range(count - 1)])
    below = lax.ppermute(upper, SLAB, [(i + 1, i) for i in range(count - 1)])
    return above, below


def exchange(cells, axes):
    return lax.all_to_all(cells, axes, split_axis=0, concat_axis=0, tiled=True)


def coded(values):
    top = jnp.max(jnp.abs(values), axis=tuple(range(values.ndim)), keepdims=True)
    exponent = jnp.ceil(jnp.log2(top + TINY))
    return jnp.round(values * (jnp.exp2(-exponent) * STEPS)), exponent


def decoded_scale(exponents):
    return jnp.exp2(exponents.astype(F32)) * (1.0 / STEPS)


def framed(piece, mark):
    steps, exponent = coded(piece)
    row = lax.broadcasted_iota(jnp.int32, (8, 128), 0)
    tail = jnp.where(row == 0, mark, exponent)
    return jnp.concatenate([steps, tail], axis=0).astype(I16)


def unframed(wide):
    return wide[:-8] * (jnp.exp2(wide[-1:]) * (1.0 / STEPS))


def shifted_columns(block, across, tap):
    if tap == 1:
        return block
    count = block.shape[0]
    wide = block.astype(F32)
    column = lax.broadcasted_iota(jnp.int32, block.shape, 0) % across
    if tap == 0:
        wide = jnp.where(column == 0, 0.0, pltpu.roll(wide, 1, 0))
    else:
        wide = jnp.where(column == across - 1, 0.0, pltpu.roll(wide, count - 1, 0))
    return wide.astype(block.dtype)


def call(body, outs, *args, flops=0, scratch=()):
    size = sum(math.prod(a.shape) * a.dtype.itemsize for a in args) + sum(
        math.prod(o.shape) * o.dtype.itemsize for o in outs
    )
    return pl.pallas_call(
        body,
        in_specs=[pl.BlockSpec(memory_space=pltpu.SMEM)]
        + [pl.BlockSpec(memory_space=pltpu.VMEM)] * (len(args) - 1),
        out_specs=[pl.BlockSpec(memory_space=pltpu.VMEM)] * len(outs),
        out_shape=list(outs),
        scratch_shapes=list(scratch),
        cost_estimate=pl.CostEstimate(flops=flops, bytes_accessed=size, transcendentals=0),
        compiler_params=pltpu.CompilerParams(vmem_limit_bytes=VMEM_LIMIT),
    )(*args)


def shift_source(section, pair, other, own, above, below, across):
    frames, rows, count, channels = own.shape

    def body(section_ref, pair_ref, other_ref, own_ref, above_ref, below_ref, out_ref):
        def write(frame, row, block):
            for tap in range(3):
                out_ref[tap, frame, row] = shifted_columns(block, across, tap)

        @pl.when(section_ref[0] == 0)
        def _():
            for frame in range(frames):
                write(frame, 0, above_ref[frame])
                for row in range(rows):
                    write(frame, row + 1, own_ref[frame, row])
                write(frame, rows + 1, below_ref[frame])

        @pl.when(section_ref[0] == 1)
        def _():
            for frame in range(frames):
                for row in range(2):
                    write(frame, row, other_ref[frame, row])
                    write(frame, row + 2, pair_ref[frame, row])

    out = jax.ShapeDtypeStruct((3, frames, rows + 2, count, channels), BF16)
    return call(body, [out], section, pair, other, own, above, below)[0]


def turn_source(section, source):
    taps, frames, rows, count, channels = source.shape

    def body(section_ref, source_ref, out_ref):
        for tap in range(taps):
            for frame in range(frames):
                for row in range(rows):
                    start = (frame * rows + row) * count
                    out_ref[tap, :, start : start + count] = source_ref[tap, frame, row].T

    out = jax.ShapeDtypeStruct((taps, channels, frames * rows * count), BF16)
    return call(body, [out], section, source)[0]


def tap_index(section_ref, row_tap, column_tap):
    decoder = section_ref[0] == 1
    return jnp.where(decoder, column_tap, row_tap), jnp.where(decoder, row_tap, column_tap)


def convolve(section, source, kernel, cotangent):
    _, frames, rimmed, count, channels = source.shape
    rows = rimmed - 2
    span = rows * count

    def body(section_ref, source_ref, kernel_ref, cot_ref, pre_ref, grad_ref):
        for frame in range(frames):
            acc = jnp.zeros((span, channels), F32)
            for r in range(3):
                for q in range(3):
                    i, j = tap_index(section_ref, r, q)
                    for back in range(frame + 1):
                        cells = source_ref[q, frame - back, r : r + rows].reshape(span, channels)
                        acc += jnp.dot(
                            cells, kernel_ref[1 - back, i, j], preferred_element_type=F32
                        )
            pre_ref[frame] = acc
            grad_ref[frame] = (cot_ref[frame].astype(F32) * silu_slope(acc)).astype(BF16)

    shape = (frames, span, channels)
    return call(
        body,
        [jax.ShapeDtypeStruct(shape, F32), jax.ShapeDtypeStruct(shape, BF16)],
        section,
        source,
        kernel,
        cotangent,
        flops=54 * span * channels * channels,
    )


def convolve_back(section, grad, above, below, kernel, across):
    frames, rows, count, channels = grad.shape
    span = rows * count

    def body(section_ref, grad_ref, above_ref, below_ref, kernel_ref, out_ref, shifted):
        for frame in range(frames):
            blocks = [above_ref[frame]] + [grad_ref[frame, r] for r in range(rows)]
            for row, block in enumerate(blocks + [below_ref[frame]]):
                for tap in range(3):
                    shifted[tap, frame, row] = shifted_columns(block, across, tap)
        for frame in range(frames):
            acc = jnp.zeros((span, channels), F32)
            for r in range(3):
                for q in range(3):
                    i, j = tap_index(section_ref, r, q)
                    for ahead in range(frames - frame):
                        cells = shifted[2 - q, frame + ahead, 2 - r : 2 - r + rows]
                        acc += lax.dot_general(
                            cells.reshape(span, channels),
                            kernel_ref[1 - ahead, i, j],
                            (((1,), (1,)), ((), ())),
                            preferred_element_type=F32,
                        )
            out_ref[frame] = acc.astype(BF16).reshape(rows, count, channels)

    return call(
        body,
        [jax.ShapeDtypeStruct(grad.shape, BF16)],
        section,
        grad,
        above,
        below,
        kernel,
        flops=54 * span * channels * channels,
        scratch=[pltpu.VMEM((3, frames, rows + 2, count, channels), BF16)],
    )[0]


def kernel_grads(section, turned, pre_act, dec_grad, returned, pair, other, parts):
    _, channels, _ = turned.shape
    frames, rows, count, _ = returned.shape
    span = rows * count
    size = channels // parts

    def body(
        section_ref, turned_ref, pre_ref, dec_ref, returned_ref, pair_ref, other_ref,
        out_ref, side, grads,
    ):
        @pl.when(section_ref[0] == 0)
        def _():
            for frame in range(frames):
                for row, quant in enumerate((pair_ref[frame, 1], other_ref[frame, 0])):
                    at = slice(row * count, (row + 1) * count)
                    side[frame, at] = (
                        returned_ref[frame, row].astype(F32)
                        + COMMIT * (pre_ref[frame, at] - quant.astype(F32))
                    ).astype(BF16)

        @pl.when(section_ref[0] == 1)
        def _():
            side[...] = dec_ref[...]

        top = jnp.zeros((8, channels), F32)
        for r in range(3):
            for q in range(3):
                i, j = tap_index(section_ref, r, q)
                tap = i * 3 + j
                first = turned_ref[q, :, r * count : r * count + span]
                start = (rows + 2 + r) * count
                second = turned_ref[q, :, start : start + span]
                late = jnp.dot(first, side[1], preferred_element_type=F32)
                same = jnp.dot(first, side[0], preferred_element_type=F32)
                same += jnp.dot(second, side[1], preferred_element_type=F32)
                for at, values in ((tap, late), (9 + tap, same)):
                    grads[at] = values
                    seen = jnp.max(jnp.abs(values).reshape(-1, 8, channels), axis=0)
                    top = jnp.maximum(top, seen)
        exponent = jnp.ceil(jnp.log2(jnp.max(top, axis=(0, 1), keepdims=True) + TINY))
        factor = jnp.exp2(-exponent) * STEPS

        @pl.loop(0, 18)
        def _(tap):
            steps = jnp.round(grads[tap] * factor).astype(I16)
            out_ref[:, tap] = steps.reshape(parts, size, channels)

        tail = jnp.broadcast_to(exponent, (size, channels)).astype(I16)
        for part in range(parts):
            out_ref[part, 18] = tail

    return call(
        body,
        [jax.ShapeDtypeStruct((parts, 19, size, channels), I16)],
        section,
        turned,
        pre_act,
        dec_grad,
        returned,
        pair,
        other,
        flops=54 * span * channels * channels,
        scratch=[
            pltpu.VMEM((frames, span, channels), BF16),
            pltpu.VMEM((18, channels, channels), F32),
        ],
    )[0]


def sum_plane(crowded, packed, pieces):
    senders, taps, size, outs = packed.shape
    taps = taps - 1
    half = taps // 2

    def body(crowded_ref, packed_ref, framed_ref, total):
        mark = jnp.full((1, 128), crowded_ref[0])
        scales = [decoded_scale(packed_ref[s, taps])[:1, :1] for s in range(senders)]
        for tap in range(taps):
            acc = packed_ref[0, tap].astype(F32) * scales[0]
            for s in range(1, senders):
                acc += packed_ref[s, tap].astype(F32) * scales[s]
            total[tap] = acc
        place = 0
        for frame in range(2):
            for oct_ in range(size // 8):
                for lane in range(outs // 128):
                    piece = total[
                        frame * half : (frame + 1) * half,
                        oct_ * 8 : oct_ * 8 + 8,
                        lane * 128 : lane * 128 + 128,
                    ]
                    framed_ref[place] = framed(piece.reshape(half * 8, 128), mark)
                    place += 1

    return pl.pallas_call(
        body,
        in_specs=[
            pl.BlockSpec(memory_space=pltpu.SMEM),
            pl.BlockSpec(memory_space=pltpu.VMEM),
        ],
        out_shape=jax.ShapeDtypeStruct((pieces, half * 8 + 8, 128), I16),
        scratch_shapes=[pltpu.VMEM((taps, size, outs), F32)],
        compiler_params=pltpu.CompilerParams(vmem_limit_bytes=VMEM_LIMIT),
    )(crowded, packed)


def sum_line(framed_parts, factor):
    def body(parts_ref, out_ref):
        first = parts_ref[0].astype(F32)
        acc, mark = unframed(first), first[-8:-7]
        for s in range(1, framed_parts.shape[0]):
            part = parts_ref[s].astype(F32)
            acc += unframed(part)
            mark = jnp.maximum(mark, part[-8:-7])
        result = framed(acc * factor, mark)
        for s in range(framed_parts.shape[0]):
            out_ref[s] = result

    return pl.pallas_call(
        body, out_shape=jax.ShapeDtypeStruct(framed_parts.shape, I16)
    )(framed_parts)


def unpack(plane, channels):
    parts, pieces, rows, _ = plane.shape
    size = channels // parts
    group = 4

    def body(plane_ref, out_ref):
        for part in range(group):
            place = 0
            for frame in range(2):
                for oct_ in range(size // 8):
                    for lane in range(channels // 128):
                        piece = unframed(plane_ref[part, place].astype(F32)).reshape(3, 3, 8, 128)
                        row = part * size + oct_ * 8
                        out_ref[frame, :, :, row : row + 8, lane * 128 : lane * 128 + 128] = piece
                        place += 1

    return pl.pallas_call(
        body,
        grid=(parts // group,),
        in_specs=[pl.BlockSpec((group, pieces, rows, 128), lambda k: (k, 0, 0, 0))],
        out_specs=pl.BlockSpec((2, 3, 3, group * size, channels), lambda k: (0, 0, 0, k, 0)),
        out_shape=jax.ShapeDtypeStruct((2, 3, 3, channels, channels), F32),
        compiler_params=pltpu.CompilerParams(vmem_limit_bytes=VMEM_LIMIT),
    )(plane)


def routed(codebook, shifted, holder, slots, turned, above, below):
    section_id = lax.axis_index("section")
    slab_id = lax.axis_index(SLAB)
    near = lax.axis_index("zh")
    plane_id = lax.axis_index(PLANE)
    planes = lax.axis_size(PLANE)
    book, channels = codebook.shape
    positions = shifted.shape[1]

    half = book // 2
    got = lax.ppermute(
        lax.dynamic_slice_in_dim(codebook, section_id * half, half, 0), "zh", [(0, 1), (1, 0)]
    )
    table = jnp.concatenate(
        [codebook, got, lax.ppermute(got, "section", [(0, 1), (1, 0)])], axis=0
    )

    before = (
        lax.broadcasted_iota(jnp.int32, (positions, positions), 0)
        < lax.broadcasted_iota(jnp.int32, (positions, positions), 1)
    ).astype(BF16)

    start = near * planes + section_id
    wanted = lax.dynamic_slice_in_dim(shifted, start, planes, 0)
    mine = lax.dynamic_slice_in_dim(holder, start, planes, 0) == plane_id
    rank = jnp.dot(mine.astype(BF16), before, preferred_element_type=F32).astype(jnp.int32)
    rank = jnp.where(mine, rank, -1)
    within = wanted % book
    far = book + jnp.where(within // half == section_id, 0, half) + within % half
    local = jnp.where(wanted // book == slab_id, within, far)
    slot_ids = lax.broadcasted_iota(jnp.int32, (1, slots, 1), 1)
    asked = jnp.sum(jnp.where(rank[:, None, :] == slot_ids, local[:, None, :], 0), axis=-1)
    picks = (
        asked.reshape(-1, 1) == lax.broadcasted_iota(jnp.int32, (1, 2 * book), 1)
    ).astype(BF16)
    table, turned, above, below = lax.optimization_barrier((table, turned, above, below))
    words = jnp.dot(picks, table, preferred_element_type=F32).astype(BF16)
    looked = exchange(words.reshape(planes, slots, channels), PLANE)
    looked = looked.reshape(planes * slots, channels)

    own_wanted = lax.dynamic_index_in_dim(shifted, slab_id + section_id, 0, keepdims=False)
    own_holder = lax.dynamic_index_in_dim(holder, slab_id + section_id, 0, keepdims=False)
    from_each = own_holder[None, :] == lax.broadcasted_iota(jnp.int32, (planes, 1), 0)
    order = jnp.dot(from_each.astype(BF16), before, preferred_element_type=F32).astype(jnp.int32)
    order = jnp.sum(jnp.where(from_each, order, 0), axis=0)
    order = jnp.where(own_wanted >= 0, own_holder * slots + order, -1)
    gather = (
        order[:, None] == lax.broadcasted_iota(jnp.int32, (1, planes * slots), 1)
    ).astype(BF16)
    pair = jnp.dot(gather, looked, preferred_element_type=F32).astype(BF16)
    return pair, turned, above, below


def front(own_field, codebook, codes, whole):
    section_id = lax.axis_index("section")
    slab_id = lax.axis_index(SLAB)
    slabs = lax.axis_size(SLAB)
    planes = lax.axis_size(PLANE)
    row_count, batch_count, frame_count, across, channels = own_field.shape
    book = codebook.shape[0]
    positions = row_count * batch_count * frame_count * across
    mean = positions // planes
    slots = int(mean + 6 * math.sqrt(mean) + 15) // 16 * 16
    cells = (frame_count, row_count, batch_count * across, channels)

    turned = own_field.reshape(row_count, batch_count, frame_count, slabs, row_count, channels)
    turned = jnp.transpose(turned, (3, 2, 4, 1, 0, 5)).reshape(slabs, -1, channels)
    turned = exchange(turned, SLAB).reshape(positions, channels)

    own = jnp.transpose(own_field, (2, 0, 1, 3, 4)).reshape(cells)
    above, below = neighbours(own[:, -1], own[:, 0])

    edge = jnp.full((1,) + codes.shape[1:], -1, codes.dtype)
    shifted = jnp.concatenate([edge, codes, edge], axis=0)
    shifted = shifted.reshape(slabs + 1, row_count, batch_count, frame_count, across)
    shifted = jnp.transpose(shifted, (0, 3, 1, 2, 4)).reshape(slabs + 1, positions)
    holder = jnp.where(shifted >= 0, shifted // book % planes, -1)

    if whole:
        wanted = lax.dynamic_index_in_dim(shifted, slab_id + section_id, 0, keepdims=False)
        every = lax.all_gather(codebook, SLAB, axis=0, tiled=True)
        taken = jnp.take(every, jnp.maximum(wanted, 0), axis=0)
        pair = jnp.where(wanted[:, None] >= 0, taken, 0).astype(BF16)
    else:
        pair, turned, above, below = routed(
            codebook, shifted, holder, slots, turned, above, below
        )

    place = lax.broadcasted_iota(jnp.int32, (positions, 1), 0)
    group, column = place // across, place % across
    place = (column // row_count) * (positions // slabs) + group * row_count + column % row_count
    sent = (place == lax.broadcasted_iota(jnp.int32, (1, positions), 1)).astype(BF16)
    cotangent = jnp.dot(sent, turned, preferred_element_type=F32).astype(BF16)

    counts = jnp.sum(
        (holder[:, None, :] == lax.broadcasted_iota(jnp.int32, (1, planes, 1), 1)).astype(F32), axis=-1
    )
    crowded = (jnp.max(counts) > slots).astype(F32).reshape(1)

    other = lax.ppermute(pair, "section", [(0, 1), (1, 0)])
    return (
        pair.reshape(cells),
        other.reshape(cells),
        cotangent.reshape(frame_count, -1, channels),
        own,
        above,
        below,
        crowded,
    )


def line_shares(fields, kernels, codebook, codes, whole):
    section = lax.axis_index("section").reshape(1).astype(jnp.int32)
    slabs = lax.axis_size(SLAB)
    own_field = fields[0]
    kernel = kernels[0]
    row_count, batch_count, frame_count, across, channels = own_field.shape
    cells = (frame_count, row_count, batch_count * across, channels)
    pair, other, cotangent, own, above, below, crowded = front(own_field, codebook, codes, whole)
    source = shift_source(section, pair, other, own, above, below, across)
    pre_act, dec_grad = convolve(section, source, kernel, cotangent)

    shaped = dec_grad.reshape(cells)
    above, below = neighbours(shaped[:, -1], shaped[:, 0])
    source = turn_source(section, source)
    back_dec = convolve_back(section, shaped, above, below, kernel, across)
    returned = lax.ppermute(back_dec, "section", [(1, 0)])

    total = (
        row_count * slabs * across * batch_count * lax.axis_size("dp") * frame_count
    )
    packed = kernel_grads(
        section, source, pre_act, dec_grad, returned, pair, other, lax.axis_size(PLANE)
    )
    plane = exchange(packed, PLANE)
    line = exchange(sum_plane(crowded, plane, lax.axis_size(Z)), Z)
    return exchange(sum_line(line, 1.0 / math.sqrt(total)), Z)


def on_device(fields, kernels, codebook, codes):
    line = line_shares(fields, kernels, codebook, codes, False)
    line = lax.cond(
        jnp.max(line[:, -8]) > 0,
        lambda frames, *args: line_shares(*args, True),
        lambda frames, *args: frames,
        line,
        fields,
        kernels,
        codebook,
        codes,
    )
    planes = lax.axis_size(PLANE)
    plane = exchange(jnp.broadcast_to(line[None], (planes,) + line.shape), PLANE)
    return unpack(plane, kernels.shape[-1])[None]


def solution(mesh):
    sections, slabs, dps = (mesh.shape[a] for a in ("section", "slab", "dp"))
    nx = 4 if slabs >= 16 else 2
    inner = Mesh(
        mesh.devices.reshape(sections, slabs // (nx * nx), nx, nx, dps),
        ("section", "zh", "y", "x", "dp"),
    )
    placed = (
        P("section", SLAB, "dp", None, None, None),
        P("section", None, None, None, None, None),
        P(SLAB, None),
        P(None, "dp", None, None),
    )
    return jax.shard_map(
        on_device,
        mesh=inner,
        in_specs=placed,
        out_specs=P("section", None, None, None, None, None),
        check_vma=False,
    )
```

```python
import math

import jax
import jax.numpy as jnp
from jax import lax
from jax.experimental import pallas as pl
from jax.experimental.pallas import tpu as pltpu
from jax.sharding import Mesh, PartitionSpec as P

COMMIT = 0.5
SLAB = ("zh", "y", "x")
PLANE = ("y", "x")
Z = ("zh", "dp")
F32 = jnp.float32
BF16 = jnp.bfloat16
I16 = jnp.int16
TINY = 2.0**-100
STEPS = 32000.0
VMEM_LIMIT = 24 * 1024 * 1024


def silu_slope(pre_act):
    sig = jax.nn.sigmoid(pre_act)
    return sig * (1.0 + pre_act * (1.0 - sig))


def neighbours(lower, upper):
    count = lax.axis_size(SLAB)
    above = lax.ppermute(lower, SLAB, [(i, i + 1) for i in range(count - 1)])
    below = lax.ppermute(upper, SLAB, [(i + 1, i) for i in range(count - 1)])
    return above, below


def exchange(cells, axes):
    return lax.all_to_all(cells, axes, split_axis=0, concat_axis=0, tiled=True)


def coded(values):
    top = jnp.max(jnp.abs(values), axis=tuple(range(values.ndim)), keepdims=True)
    exponent = jnp.ceil(jnp.log2(top + TINY))
    return jnp.round(values * (jnp.exp2(-exponent) * STEPS)), exponent


def decoded_scale(exponents):
    return jnp.exp2(exponents.astype(F32)) * (1.0 / STEPS)


def framed(piece, mark):
    steps, exponent = coded(piece)
    row = lax.broadcasted_iota(jnp.int32, (8, 128), 0)
    tail = jnp.where(row == 0, mark, exponent)
    return jnp.concatenate([steps, tail], axis=0).astype(I16)


def unframed(wide):
    return wide[:-8] * (jnp.exp2(wide[-1:]) * (1.0 / STEPS))


def shifted_columns(block, across, tap):
    if tap == 1:
        return block
    count = block.shape[0]
    wide = block.astype(F32)
    column = lax.broadcasted_iota(jnp.int32, block.shape, 0) % across
    if tap == 0:
        wide = jnp.where(column == 0, 0.0, pltpu.roll(wide, 1, 0))
    else:
        wide = jnp.where(column == across - 1, 0.0, pltpu.roll(wide, count - 1, 0))
    return wide.astype(block.dtype)


def call(body, outs, *args, flops=0, scratch=()):
    size = sum(math.prod(a.shape) * a.dtype.itemsize for a in args) + sum(
        math.prod(o.shape) * o.dtype.itemsize for o in outs
    )
    return pl.pallas_call(
        body,
        in_specs=[pl.BlockSpec(memory_space=pltpu.SMEM)]
        + [pl.BlockSpec(memory_space=pltpu.VMEM)] * (len(args) - 1),
        out_specs=[pl.BlockSpec(memory_space=pltpu.VMEM)] * len(outs),
        out_shape=list(outs),
        scratch_shapes=list(scratch),
        cost_estimate=pl.CostEstimate(flops=flops, bytes_accessed=size, transcendentals=0),
        compiler_params=pltpu.CompilerParams(vmem_limit_bytes=VMEM_LIMIT),
    )(*args)


def shift_source(section, pair, other, across):
    frames, rows, count, channels = pair.shape

    def body(section_ref, pair_ref, other_ref, out_ref):
        @pl.when(section_ref[0] == 1)
        def _():
            for frame in range(frames):
                for row in range(rows):
                    for tap in range(3):
                        block = shifted_columns(other_ref[frame, row], across, tap)
                        out_ref[tap, frame, row] = block
                        block = shifted_columns(pair_ref[frame, row], across, tap)
                        out_ref[tap, frame, rows + row] = block

    out = jax.ShapeDtypeStruct((3, frames, 2 * rows, count, channels), BF16)
    return call(body, [out], section, pair, other)[0]


def rimmed_block(frame, row, above_ref, cells_ref, below_ref):
    rows = cells_ref.shape[1]
    if row == 0:
        return above_ref[frame]
    return below_ref[frame] if row > rows else cells_ref[frame, row - 1]


def turn_source(section, source, cells, above, below, across):
    taps, frames, rows, count, channels = source.shape

    def body(section_ref, source_ref, cells_ref, above_ref, below_ref, out_ref):
        def write(block_of):
            for frame in range(frames):
                for row in range(rows):
                    start = (frame * rows + row) * count
                    for tap in range(taps):
                        out_ref[tap, :, start : start + count] = block_of(tap, frame, row).T

        def encoder_block(tap, frame, row):
            block = rimmed_block(frame, row, above_ref, cells_ref, below_ref)
            return shifted_columns(block, across, tap)

        @pl.when(section_ref[0] == 0)
        def _():
            write(encoder_block)

        @pl.when(section_ref[0] == 1)
        def _():
            write(lambda tap, frame, row: source_ref[tap, frame, row])

    out = jax.ShapeDtypeStruct((taps, channels, frames * rows * count), BF16)
    return call(body, [out], section, source, cells, above, below)[0]


def tap_index(section_ref, row_tap, column_tap):
    decoder = section_ref[0] == 1
    return jnp.where(decoder, column_tap, row_tap), jnp.where(decoder, row_tap, column_tap)


def convolved(section_ref, source_ref, kernel_ref, frame):
    _, _, rimmed, count, channels = source_ref.shape
    rows = rimmed - 2
    acc = jnp.zeros((rows * count, channels), F32)
    for r in range(3):
        for q in range(3):
            i, j = tap_index(section_ref, r, q)
            for back in range(frame + 1):
                cells = source_ref[q, frame - back, r : r + rows].reshape(rows * count, channels)
                acc += jnp.dot(cells, kernel_ref[1 - back, i, j], preferred_element_type=F32)
    return acc


def decoder_grad(section, source, kernel, cotangent, own):
    frames, rows, count, channels = own.shape

    def body(section_ref, source_ref, kernel_ref, cot_ref, own_ref, out_ref):
        @pl.when(section_ref[0] == 0)
        def _():
            out_ref[...] = own_ref[...]

        @pl.when(section_ref[0] == 1)
        def _():
            for frame in range(frames):
                slope = silu_slope(convolved(section_ref, source_ref, kernel_ref, frame))
                grad = (cot_ref[frame].astype(F32) * slope).astype(BF16)
                out_ref[frame] = grad.reshape(rows, count, channels)

    return call(
        body,
        [jax.ShapeDtypeStruct(own.shape, BF16)],
        section,
        source,
        kernel,
        cotangent,
        own,
        flops=54 * rows * count * channels * channels,
    )[0]


def back_and_forth(section, cells, above, below, kernel, across):
    frames, rows, count, channels = cells.shape
    span = rows * count

    def body(
        section_ref, cells_ref, above_ref, below_ref, kernel_ref, back_ref, pre_ref, shifted
    ):
        for frame in range(frames):
            for row in range(rows + 2):
                block = rimmed_block(frame, row, above_ref, cells_ref, below_ref)
                for tap in range(3):
                    shifted[tap, frame, row] = shifted_columns(block, across, tap)

        @pl.when(section_ref[0] == 0)
        def _():
            for frame in range(frames):
                pre_ref[frame] = convolved(section_ref, shifted, kernel_ref, frame)

        @pl.when(section_ref[0] == 1)
        def _():
            for frame in range(frames):
                acc = jnp.zeros((span, channels), F32)
                for r in range(3):
                    for q in range(3):
                        i, j = tap_index(section_ref, r, q)
                        for ahead in range(frames - frame):
                            grads = shifted[2 - q, frame + ahead, 2 - r : 2 - r + rows]
                            acc += lax.dot_general(
                                grads.reshape(span, channels),
                                kernel_ref[1 - ahead, i, j],
                                (((1,), (1,)), ((), ())),
                                preferred_element_type=F32,
                            )
                back_ref[frame] = acc.astype(BF16).reshape(rows, count, channels)

    return call(
        body,
        [
            jax.ShapeDtypeStruct(cells.shape, BF16),
            jax.ShapeDtypeStruct((frames, span, channels), F32),
        ],
        section,
        cells,
        above,
        below,
        kernel,
        flops=54 * span * channels * channels,
        scratch=[pltpu.VMEM((3, frames, rows + 2, count, channels), BF16)],
    )


def kernel_grads(section, turned, pre_act, dec_grad, returned, pair, other, parts):
    _, channels, _ = turned.shape
    frames, rows, count, _ = returned.shape
    span = rows * count
    size = channels // parts

    def body(
        section_ref, turned_ref, pre_ref, dec_ref, returned_ref, pair_ref, other_ref,
        out_ref, side, grads,
    ):
        @pl.when(section_ref[0] == 0)
        def _():
            for frame in range(frames):
                for row, quant in enumerate((pair_ref[frame, 1], other_ref[frame, 0])):
                    at = slice(row * count, (row + 1) * count)
                    side[frame, at] = (
                        returned_ref[frame, row].astype(F32)
                        + COMMIT * (pre_ref[frame, at] - quant.astype(F32))
                    ).astype(BF16)

        @pl.when(section_ref[0] == 1)
        def _():
            side[...] = dec_ref[...].reshape(frames, span, channels)

        top = jnp.zeros((8, channels), F32)
        for r in range(3):
            for q in range(3):
                i, j = tap_index(section_ref, r, q)
                tap = i * 3 + j
                first = turned_ref[q, :, r * count : r * count + span]
                start = (rows + 2 + r) * count
                second = turned_ref[q, :, start : start + span]
                late = jnp.dot(first, side[1], preferred_element_type=F32)
                same = jnp.dot(first, side[0], preferred_element_type=F32)
                same += jnp.dot(second, side[1], preferred_element_type=F32)
                for at, values in ((tap, late), (9 + tap, same)):
                    grads[at] = values
                    seen = jnp.max(jnp.abs(values).reshape(-1, 8, channels), axis=0)
                    top = jnp.maximum(top, seen)
        exponent = jnp.ceil(jnp.log2(jnp.max(top, axis=(0, 1), keepdims=True) + TINY))
        factor = jnp.exp2(-exponent) * STEPS

        @pl.loop(0, 18)
        def _(tap):
            steps = jnp.round(grads[tap] * factor).astype(I16)
            out_ref[:, tap] = steps.reshape(parts, size, channels)

        tail = jnp.broadcast_to(exponent, (size, channels)).astype(I16)
        for part in range(parts):
            out_ref[part, 18] = tail

    return call(
        body,
        [jax.ShapeDtypeStruct((parts, 19, size, channels), I16)],
        section,
        turned,
        pre_act,
        dec_grad,
        returned,
        pair,
        other,
        flops=54 * span * channels * channels,
        scratch=[
            pltpu.VMEM((frames, span, channels), BF16),
            pltpu.VMEM((18, channels, channels), F32),
        ],
    )[0]


def sum_plane(crowded, packed, pieces):
    senders, taps, size, outs = packed.shape
    taps = taps - 1
    half = taps // 2

    def body(crowded_ref, packed_ref, framed_ref, total):
        mark = jnp.full((1, 128), crowded_ref[0])
        scales = [decoded_scale(packed_ref[s, taps])[:1, :1] for s in range(senders)]
        for tap in range(taps):
            acc = packed_ref[0, tap].astype(F32) * scales[0]
            for s in range(1, senders):
                acc += packed_ref[s, tap].astype(F32) * scales[s]
            total[tap] = acc
        place = 0
        for frame in range(2):
            for oct_ in range(size // 8):
                for lane in range(outs // 128):
                    piece = total[
                        frame * half : (frame + 1) * half,
                        oct_ * 8 : oct_ * 8 + 8,
                        lane * 128 : lane * 128 + 128,
                    ]
                    framed_ref[place] = framed(piece.reshape(half * 8, 128), mark)
                    place += 1

    return pl.pallas_call(
        body,
        in_specs=[
            pl.BlockSpec(memory_space=pltpu.SMEM),
            pl.BlockSpec(memory_space=pltpu.VMEM),
        ],
        out_shape=jax.ShapeDtypeStruct((pieces, half * 8 + 8, 128), I16),
        scratch_shapes=[pltpu.VMEM((taps, size, outs), F32)],
        compiler_params=pltpu.CompilerParams(vmem_limit_bytes=VMEM_LIMIT),
    )(crowded, packed)


def sum_line(framed_parts, factor):
    def body(parts_ref, out_ref):
        first = parts_ref[0].astype(F32)
        acc, mark = unframed(first), first[-8:-7]
        for s in range(1, framed_parts.shape[0]):
            part = parts_ref[s].astype(F32)
            acc += unframed(part)
            mark = jnp.maximum(mark, part[-8:-7])
        result = framed(acc * factor, mark)
        for s in range(framed_parts.shape[0]):
            out_ref[s] = result

    return pl.pallas_call(
        body, out_shape=jax.ShapeDtypeStruct(framed_parts.shape, I16)
    )(framed_parts)


def unpack(plane, channels):
    parts, pieces, rows, _ = plane.shape
    size = channels // parts
    group = 4

    def body(plane_ref, out_ref):
        for part in range(group):
            place = 0
            for frame in range(2):
                for oct_ in range(size // 8):
                    for lane in range(channels // 128):
                        piece = unframed(plane_ref[part, place].astype(F32)).reshape(3, 3, 8, 128)
                        row = part * size + oct_ * 8
                        out_ref[frame, :, :, row : row + 8, lane * 128 : lane * 128 + 128] = piece
                        place += 1

    return pl.pallas_call(
        body,
        grid=(parts // group,),
        in_specs=[pl.BlockSpec((group, pieces, rows, 128), lambda k: (k, 0, 0, 0))],
        out_specs=pl.BlockSpec((2, 3, 3, group * size, channels), lambda k: (0, 0, 0, k, 0)),
        out_shape=jax.ShapeDtypeStruct((2, 3, 3, channels, channels), F32),
        compiler_params=pltpu.CompilerParams(vmem_limit_bytes=VMEM_LIMIT),
    )(plane)


def routed(codebook, shifted, holder, slots, turned):
    section_id = lax.axis_index("section")
    slab_id = lax.axis_index(SLAB)
    near = lax.axis_index("zh")
    plane_id = lax.axis_index(PLANE)
    planes = lax.axis_size(PLANE)
    book, channels = codebook.shape
    positions = shifted.shape[1]

    half = book // 2
    got = lax.ppermute(
        lax.dynamic_slice_in_dim(codebook, section_id * half, half, 0), "zh", [(0, 1), (1, 0)]
    )
    table = jnp.concatenate(
        [codebook, got, lax.ppermute(got, "section", [(0, 1), (1, 0)])], axis=0
    )

    before = (
        lax.broadcasted_iota(jnp.int32, (positions, positions), 0)
        < lax.broadcasted_iota(jnp.int32, (positions, positions), 1)
    ).astype(BF16)

    start = near * planes + section_id
    wanted = lax.dynamic_slice_in_dim(shifted, start, planes, 0)
    mine = lax.dynamic_slice_in_dim(holder, start, planes, 0) == plane_id
    rank = jnp.dot(mine.astype(BF16), before, preferred_element_type=F32).astype(jnp.int32)
    rank = jnp.where(mine, rank, -1)
    within = wanted % book
    far = book + jnp.where(within // half == section_id, 0, half) + within % half
    local = jnp.where(wanted // book == slab_id, within, far)
    slot_ids = lax.broadcasted_iota(jnp.int32, (1, slots, 1), 1)
    asked = jnp.sum(jnp.where(rank[:, None, :] == slot_ids, local[:, None, :], 0), axis=-1)
    picks = (
        asked.reshape(-1, 1) == lax.broadcasted_iota(jnp.int32, (1, 2 * book), 1)
    ).astype(BF16)
    table, turned = lax.optimization_barrier((table, turned))
    words = jnp.dot(picks, table, preferred_element_type=F32).astype(BF16)
    looked = exchange(words.reshape(planes, slots, channels), PLANE)
    looked = looked.reshape(planes * slots, channels)

    own_wanted = lax.dynamic_index_in_dim(shifted, slab_id + section_id, 0, keepdims=False)
    own_holder = lax.dynamic_index_in_dim(holder, slab_id + section_id, 0, keepdims=False)
    from_each = own_holder[None, :] == lax.broadcasted_iota(jnp.int32, (planes, 1), 0)
    order = jnp.dot(from_each.astype(BF16), before, preferred_element_type=F32).astype(jnp.int32)
    order = jnp.sum(jnp.where(from_each, order, 0), axis=0)
    order = jnp.where(own_wanted >= 0, own_holder * slots + order, -1)
    gather = (
        order[:, None] == lax.broadcasted_iota(jnp.int32, (1, planes * slots), 1)
    ).astype(BF16)
    pair = jnp.dot(gather, looked, preferred_element_type=F32).astype(BF16)
    return pair, turned


def front(own_field, codebook, codes, whole):
    section_id = lax.axis_index("section")
    slab_id = lax.axis_index(SLAB)
    slabs = lax.axis_size(SLAB)
    planes = lax.axis_size(PLANE)
    row_count, batch_count, frame_count, across, channels = own_field.shape
    book = codebook.shape[0]
    positions = row_count * batch_count * frame_count * across
    mean = positions // planes
    slots = int(mean + 6 * math.sqrt(mean) + 15) // 16 * 16
    cells = (frame_count, row_count, batch_count * across, channels)

    turned = own_field.reshape(row_count, batch_count, frame_count, slabs, row_count, channels)
    turned = jnp.transpose(turned, (3, 2, 4, 1, 0, 5)).reshape(slabs, -1, channels)
    turned = exchange(turned, SLAB).reshape(positions, channels)

    own = jnp.transpose(own_field, (2, 0, 1, 3, 4)).reshape(cells)

    edge = jnp.full((1,) + codes.shape[1:], -1, codes.dtype)
    shifted = jnp.concatenate([edge, codes, edge], axis=0)
    shifted = shifted.reshape(slabs + 1, row_count, batch_count, frame_count, across)
    shifted = jnp.transpose(shifted, (0, 3, 1, 2, 4)).reshape(slabs + 1, positions)
    holder = jnp.where(shifted >= 0, shifted // book % planes, -1)

    if whole:
        wanted = lax.dynamic_index_in_dim(shifted, slab_id + section_id, 0, keepdims=False)
        every = lax.all_gather(codebook, SLAB, axis=0, tiled=True)
        taken = jnp.take(every, jnp.maximum(wanted, 0), axis=0)
        pair = jnp.where(wanted[:, None] >= 0, taken, 0).astype(BF16)
    else:
        pair, turned = routed(codebook, shifted, holder, slots, turned)

    place = lax.broadcasted_iota(jnp.int32, (positions, 1), 0)
    group, column = place // across, place % across
    place = (column // row_count) * (positions // slabs) + group * row_count + column % row_count
    sent = (place == lax.broadcasted_iota(jnp.int32, (1, positions), 1)).astype(BF16)
    cotangent = jnp.dot(sent, turned, preferred_element_type=F32).astype(BF16)

    counts = jnp.sum(
        (holder[:, None, :] == lax.broadcasted_iota(jnp.int32, (1, planes, 1), 1)).astype(F32), axis=-1
    )
    crowded = (jnp.max(counts) > slots).astype(F32).reshape(1)

    other = lax.ppermute(pair, "section", [(0, 1), (1, 0)])
    return (
        pair.reshape(cells),
        other.reshape(cells),
        cotangent.reshape(frame_count, -1, channels),
        own,
        crowded,
    )


def line_shares(fields, kernels, codebook, codes, whole):
    section = lax.axis_index("section").reshape(1).astype(jnp.int32)
    slabs = lax.axis_size(SLAB)
    own_field = fields[0]
    kernel = kernels[0]
    row_count, batch_count, frame_count, across, channels = own_field.shape
    pair, other, cotangent, own, crowded = front(own_field, codebook, codes, whole)
    source = shift_source(section, pair, other, across)
    cells = decoder_grad(section, source, kernel, cotangent, own)
    above, below = neighbours(cells[:, -1], cells[:, 0])
    back_dec, pre_act = back_and_forth(section, cells, above, below, kernel, across)
    source = turn_source(section, source, cells, above, below, across)
    returned = lax.ppermute(back_dec, "section", [(1, 0)])

    total = (
        row_count * slabs * across * batch_count * lax.axis_size("dp") * frame_count
    )
    packed = kernel_grads(
        section, source, pre_act, cells, returned, pair, other, lax.axis_size(PLANE)
    )
    plane = exchange(packed, PLANE)
    line = exchange(sum_plane(crowded, plane, lax.axis_size(Z)), Z)
    return exchange(sum_line(line, 1.0 / math.sqrt(total)), Z)


def on_device(fields, kernels, codebook, codes):
    line = line_shares(fields, kernels, codebook, codes, False)
    line = lax.cond(
        jnp.max(line[:, -8]) > 0,
        lambda frames, *args: line_shares(*args, True),
        lambda frames, *args: frames,
        line,
        fields,
        kernels,
        codebook,
        codes,
    )
    planes = lax.axis_size(PLANE)
    plane = exchange(jnp.broadcast_to(line[None], (planes,) + line.shape), PLANE)
    return unpack(plane, kernels.shape[-1])[None]


def solution(mesh):
    sections, slabs, dps = (mesh.shape[a] for a in ("section", "slab", "dp"))
    nx = 4 if slabs >= 16 else 2
    inner = Mesh(
        mesh.devices.reshape(sections, slabs // (nx * nx), nx, nx, dps),
        ("section", "zh", "y", "x", "dp"),
    )
    placed = (
        P("section", SLAB, "dp", None, None, None),
        P("section", None, None, None, None, None),
        P(SLAB, None),
        P(None, "dp", None, None),
    )
    return jax.shard_map(
        on_device,
        mesh=inner,
        in_specs=placed,
        out_specs=P("section", None, None, None, None, None),
        check_vma=False,
    )
```

```python
import math

import jax
import jax.numpy as jnp
from jax import lax
from jax.experimental import pallas as pl
from jax.experimental.pallas import tpu as pltpu
from jax.sharding import Mesh, PartitionSpec as P

COMMIT = 0.5
SLAB = ("zh", "y", "x")
PLANE = ("y", "x")
Z = ("zh", "dp")
F32 = jnp.float32
BF16 = jnp.bfloat16
I16 = jnp.int16
TINY = 2.0**-100
STEPS = 32000.0
VMEM_LIMIT = 24 * 1024 * 1024


def silu_slope(pre_act):
    sig = jax.nn.sigmoid(pre_act)
    return sig * (1.0 + pre_act * (1.0 - sig))


def neighbours(lower, upper, own_lower, own_upper):
    slabs = lax.axis_size(SLAB)
    cut = slabs // lax.axis_size("zh")
    axes = ("section",) + SLAB
    early = [(i, i + 1) for i in range(cut - 1, slabs - 1, cut)]
    late = [(i, i + 1) for i in range(2 * slabs - 1) if i != slabs - 1 and (i, i + 1) not in early]
    above = lax.ppermute(lower, axes, late), lax.ppermute(own_lower, axes, early)
    late, early = [(j, i) for i, j in late], [(j, i) for i, j in early]
    below = lax.ppermute(upper, axes, late), lax.ppermute(own_upper, axes, early)
    return above, below


def exchange(cells, axes):
    return lax.all_to_all(cells, axes, split_axis=0, concat_axis=0, tiled=True)


def coded(values):
    top = jnp.max(jnp.abs(values), axis=tuple(range(values.ndim)), keepdims=True)
    exponent = jnp.ceil(jnp.log2(top + TINY))
    return jnp.round(values * (jnp.exp2(-exponent) * STEPS)), exponent


def decoded_scale(exponents):
    return jnp.exp2(exponents.astype(F32)) * (1.0 / STEPS)


def framed(piece, mark):
    steps, exponent = coded(piece)
    row = lax.broadcasted_iota(jnp.int32, (8, 128), 0)
    tail = jnp.where(row == 0, mark, exponent)
    return jnp.concatenate([steps, tail], axis=0).astype(I16)


def unframed(wide):
    return wide[:-8] * (jnp.exp2(wide[-1:]) * (1.0 / STEPS))


def shifted_columns(block, across, tap):
    if tap == 1:
        return block
    count = block.shape[0]
    wide = block.astype(F32)
    column = lax.broadcasted_iota(jnp.int32, block.shape, 0) % across
    if tap == 0:
        wide = jnp.where(column == 0, 0.0, pltpu.roll(wide, 1, 0))
    else:
        wide = jnp.where(column == across - 1, 0.0, pltpu.roll(wide, count - 1, 0))
    return wide.astype(block.dtype)


def call(body, outs, *args, flops=0, scratch=()):
    size = sum(math.prod(a.shape) * a.dtype.itemsize for a in args) + sum(
        math.prod(o.shape) * o.dtype.itemsize for o in outs
    )
    return pl.pallas_call(
        body,
        in_specs=[pl.BlockSpec(memory_space=pltpu.SMEM)]
        + [pl.BlockSpec(memory_space=pltpu.VMEM)] * (len(args) - 1),
        out_specs=[pl.BlockSpec(memory_space=pltpu.VMEM)] * len(outs),
        out_shape=list(outs),
        scratch_shapes=list(scratch),
        cost_estimate=pl.CostEstimate(flops=flops, bytes_accessed=size, transcendentals=0),
        compiler_params=pltpu.CompilerParams(vmem_limit_bytes=VMEM_LIMIT),
    )(*args)


def shift_source(section, pair, other, across):
    frames, rows, count, channels = pair.shape

    def body(section_ref, pair_ref, other_ref, out_ref):
        @pl.when(section_ref[0] == 1)
        def _():
            for frame in range(frames):
                for row in range(rows):
                    for tap in range(3):
                        block = shifted_columns(other_ref[frame, row], across, tap)
                        out_ref[tap, frame, row] = block
                        block = shifted_columns(pair_ref[frame, row], across, tap)
                        out_ref[tap, frame, rows + row] = block

    out = jax.ShapeDtypeStruct((3, frames, 2 * rows, count, channels), BF16)
    return call(body, [out], section, pair, other)[0]


def rimmed_block(frame, row, cells_ref, above_refs, below_refs):
    rows = cells_ref.shape[1]
    if 0 < row <= rows:
        return cells_ref[frame, row - 1]
    late, early = below_refs if row else above_refs
    return late[frame] + early[frame]


def turn_source(section, source, cells, above, below, across):
    taps, frames, rows, count, channels = source.shape

    def body(section_ref, source_ref, cells_ref, *refs):
        above_refs, below_refs, out_ref = refs[:2], refs[2:4], refs[4]

        def write(block_of):
            for frame in range(frames):
                for row in range(rows):
                    start = (frame * rows + row) * count
                    for tap in range(taps):
                        out_ref[tap, :, start : start + count] = block_of(tap, frame, row).T

        def encoder_block(tap, frame, row):
            block = rimmed_block(frame, row, cells_ref, above_refs, below_refs)
            return shifted_columns(block, across, tap)

        @pl.when(section_ref[0] == 0)
        def _():
            write(encoder_block)

        @pl.when(section_ref[0] == 1)
        def _():
            write(lambda tap, frame, row: source_ref[tap, frame, row])

    out = jax.ShapeDtypeStruct((taps, channels, frames * rows * count), BF16)
    return call(body, [out], section, source, cells, *above, *below)[0]


def tap_index(section_ref, row_tap, column_tap):
    decoder = section_ref[0] == 1
    return jnp.where(decoder, column_tap, row_tap), jnp.where(decoder, row_tap, column_tap)


def convolved(section_ref, source_ref, kernel_ref, frame):
    _, _, rimmed, count, channels = source_ref.shape
    rows = rimmed - 2
    acc = jnp.zeros((rows * count, channels), F32)
    for r in range(3):
        for q in range(3):
            i, j = tap_index(section_ref, r, q)
            for back in range(frame + 1):
                cells = source_ref[q, frame - back, r : r + rows].reshape(rows * count, channels)
                acc += jnp.dot(cells, kernel_ref[1 - back, i, j], preferred_element_type=F32)
    return acc


def decoder_grad(section, source, kernel, cotangent, own):
    frames, rows, count, channels = own.shape

    def body(section_ref, source_ref, kernel_ref, cot_ref, own_ref, out_ref):
        @pl.when(section_ref[0] == 0)
        def _():
            out_ref[...] = own_ref[...]

        @pl.when(section_ref[0] == 1)
        def _():
            for frame in range(frames):
                slope = silu_slope(convolved(section_ref, source_ref, kernel_ref, frame))
                grad = (cot_ref[frame].astype(F32) * slope).astype(BF16)
                out_ref[frame] = grad.reshape(rows, count, channels)

    return call(
        body,
        [jax.ShapeDtypeStruct(own.shape, BF16)],
        section,
        source,
        kernel,
        cotangent,
        own,
        flops=54 * rows * count * channels * channels,
    )[0]


def back_and_forth(section, cells, above, below, kernel, across):
    frames, rows, count, channels = cells.shape
    span = rows * count

    def body(section_ref, cells_ref, *refs):
        above_refs, below_refs = refs[:2], refs[2:4]
        kernel_ref, back_ref, pre_ref, shifted = refs[4:]
        for frame in range(frames):
            for row in range(rows + 2):
                block = rimmed_block(frame, row, cells_ref, above_refs, below_refs)
                for tap in range(3):
                    shifted[tap, frame, row] = shifted_columns(block, across, tap)

        @pl.when(section_ref[0] == 0)
        def _():
            for frame in range(frames):
                pre_ref[frame] = convolved(section_ref, shifted, kernel_ref, frame)

        @pl.when(section_ref[0] == 1)
        def _():
            for frame in range(frames):
                acc = jnp.zeros((span, channels), F32)
                for r in range(3):
                    for q in range(3):
                        i, j = tap_index(section_ref, r, q)
                        for ahead in range(frames - frame):
                            grads = shifted[2 - q, frame + ahead, 2 - r : 2 - r + rows]
                            acc += lax.dot_general(
                                grads.reshape(span, channels),
                                kernel_ref[1 - ahead, i, j],
                                (((1,), (1,)), ((), ())),
                                preferred_element_type=F32,
                            )
                back_ref[frame] = acc.astype(BF16).reshape(rows, count, channels)

    return call(
        body,
        [
            jax.ShapeDtypeStruct(cells.shape, BF16),
            jax.ShapeDtypeStruct((frames, span, channels), F32),
        ],
        section,
        cells,
        *above,
        *below,
        kernel,
        flops=54 * span * channels * channels,
        scratch=[pltpu.VMEM((3, frames, rows + 2, count, channels), BF16)],
    )


def kernel_grads(section, turned, pre_act, dec_grad, returned, pair, other, parts):
    _, channels, _ = turned.shape
    frames, rows, count, _ = returned.shape
    span = rows * count
    size = channels // parts

    def body(
        section_ref, turned_ref, pre_ref, dec_ref, returned_ref, pair_ref, other_ref,
        out_ref, side, grads,
    ):
        @pl.when(section_ref[0] == 0)
        def _():
            for frame in range(frames):
                for row, quant in enumerate((pair_ref[frame, 1], other_ref[frame, 0])):
                    at = slice(row * count, (row + 1) * count)
                    side[frame, at] = (
                        returned_ref[frame, row].astype(F32)
                        + COMMIT * (pre_ref[frame, at] - quant.astype(F32))
                    ).astype(BF16)

        @pl.when(section_ref[0] == 1)
        def _():
            side[...] = dec_ref[...].reshape(frames, span, channels)

        top = jnp.zeros((8, channels), F32)
        for r in range(3):
            for q in range(3):
                i, j = tap_index(section_ref, r, q)
                tap = i * 3 + j
                first = turned_ref[q, :, r * count : r * count + span]
                start = (rows + 2 + r) * count
                second = turned_ref[q, :, start : start + span]
                late = jnp.dot(first, side[1], preferred_element_type=F32)
                same = jnp.dot(first, side[0], preferred_element_type=F32)
                same += jnp.dot(second, side[1], preferred_element_type=F32)
                for at, values in ((tap, late), (9 + tap, same)):
                    grads[at] = values
                    seen = jnp.max(jnp.abs(values).reshape(-1, 8, channels), axis=0)
                    top = jnp.maximum(top, seen)
        exponent = jnp.ceil(jnp.log2(jnp.max(top, axis=(0, 1), keepdims=True) + TINY))
        factor = jnp.exp2(-exponent) * STEPS

        @pl.loop(0, 18)
        def _(tap):
            steps = jnp.round(grads[tap] * factor).astype(I16)
            out_ref[:, tap] = steps.reshape(parts, size, channels)

        tail = jnp.broadcast_to(exponent, (size, channels)).astype(I16)
        for part in range(parts):
            out_ref[part, 18] = tail

    return call(
        body,
        [jax.ShapeDtypeStruct((parts, 19, size, channels), I16)],
        section,
        turned,
        pre_act,
        dec_grad,
        returned,
        pair,
        other,
        flops=54 * span * channels * channels,
        scratch=[
            pltpu.VMEM((frames, span, channels), BF16),
            pltpu.VMEM((18, channels, channels), F32),
        ],
    )[0]


def sum_plane(crowded, packed, pieces):
    senders, taps, size, outs = packed.shape
    taps = taps - 1
    half = taps // 2

    def body(crowded_ref, packed_ref, framed_ref, total):
        mark = jnp.full((1, 128), crowded_ref[0])
        scales = [decoded_scale(packed_ref[s, taps])[:1, :1] for s in range(senders)]
        for tap in range(taps):
            acc = packed_ref[0, tap].astype(F32) * scales[0]
            for s in range(1, senders):
                acc += packed_ref[s, tap].astype(F32) * scales[s]
            total[tap] = acc
        place = 0
        for frame in range(2):
            for oct_ in range(size // 8):
                for lane in range(outs // 128):
                    piece = total[
                        frame * half : (frame + 1) * half,
                        oct_ * 8 : oct_ * 8 + 8,
                        lane * 128 : lane * 128 + 128,
                    ]
                    framed_ref[place] = framed(piece.reshape(half * 8, 128), mark)
                    place += 1

    return pl.pallas_call(
        body,
        in_specs=[
            pl.BlockSpec(memory_space=pltpu.SMEM),
            pl.BlockSpec(memory_space=pltpu.VMEM),
        ],
        out_shape=jax.ShapeDtypeStruct((pieces, half * 8 + 8, 128), I16),
        scratch_shapes=[pltpu.VMEM((taps, size, outs), F32)],
        compiler_params=pltpu.CompilerParams(vmem_limit_bytes=VMEM_LIMIT),
    )(crowded, packed)


def sum_line(framed_parts, factor):
    def body(parts_ref, out_ref):
        first = parts_ref[0].astype(F32)
        acc, mark = unframed(first), first[-8:-7]
        for s in range(1, framed_parts.shape[0]):
            part = parts_ref[s].astype(F32)
            acc += unframed(part)
            mark = jnp.maximum(mark, part[-8:-7])
        result = framed(acc * factor, mark)
        for s in range(framed_parts.shape[0]):
            out_ref[s] = result

    return pl.pallas_call(
        body, out_shape=jax.ShapeDtypeStruct(framed_parts.shape, I16)
    )(framed_parts)


def spread(line, parts):
    pieces, rows, _ = line.shape
    rows -= 8

    def body(line_ref, out_ref):
        wide = [line_ref[p].astype(F32) for p in range(pieces)]
        row = lax.broadcasted_iota(jnp.int32, (16, 128), 0)
        tail = jnp.zeros((16, 128), F32)
        for p in range(pieces):
            tail = jnp.where(row == p, wide[p][-1:], tail)
        result = jnp.concatenate([w[:-8] for w in wide] + [tail], axis=0).astype(I16)
        for part in range(parts):
            out_ref[part] = result

    return pl.pallas_call(
        body, out_shape=jax.ShapeDtypeStruct((parts, pieces * rows + 16, 128), I16)
    )(line)


def unpack(plane, channels):
    parts, rows, _ = plane.shape
    size = channels // parts
    pieces = 2 * (size // 8) * (channels // 128)
    each = (rows - 16) // pieces
    group = 4

    def body(plane_ref, out_ref):
        for part in range(group):
            wide = plane_ref[part].astype(F32)
            scales = jnp.exp2(wide[-16:]) * (1.0 / STEPS)
            place = 0
            for frame in range(2):
                for oct_ in range(size // 8):
                    for lane in range(channels // 128):
                        piece = wide[place * each : (place + 1) * each] * scales[place : place + 1]
                        row = part * size + oct_ * 8
                        out_ref[
                            frame, :, :, row : row + 8, lane * 128 : lane * 128 + 128
                        ] = piece.reshape(3, 3, 8, 128)
                        place += 1

    return pl.pallas_call(
        body,
        grid=(parts // group,),
        in_specs=[pl.BlockSpec((group, rows, 128), lambda k: (k, 0, 0))],
        out_specs=pl.BlockSpec((2, 3, 3, group * size, channels), lambda k: (0, 0, 0, k, 0)),
        out_shape=jax.ShapeDtypeStruct((2, 3, 3, channels, channels), F32),
        compiler_params=pltpu.CompilerParams(vmem_limit_bytes=VMEM_LIMIT),
    )(plane)


def routed(codebook, shifted, holder, slots, turned):
    section_id = lax.axis_index("section")
    slab_id = lax.axis_index(SLAB)
    near = lax.axis_index("zh")
    plane_id = lax.axis_index(PLANE)
    planes = lax.axis_size(PLANE)
    book, channels = codebook.shape
    positions = shifted.shape[1]

    half = book // 2
    got = lax.ppermute(
        lax.dynamic_slice_in_dim(codebook, section_id * half, half, 0), "zh", [(0, 1), (1, 0)]
    )
    table = jnp.concatenate(
        [codebook, got, lax.ppermute(got, "section", [(0, 1), (1, 0)])], axis=0
    )

    before = (
        lax.broadcasted_iota(jnp.int32, (positions, positions), 0)
        < lax.broadcasted_iota(jnp.int32, (positions, positions), 1)
    ).astype(BF16)

    start = near * planes + section_id
    wanted = lax.dynamic_slice_in_dim(shifted, start, planes, 0)
    mine = lax.dynamic_slice_in_dim(holder, start, planes, 0) == plane_id
    rank = jnp.dot(mine.astype(BF16), before, preferred_element_type=F32).astype(jnp.int32)
    rank = jnp.where(mine, rank, -1)
    within = wanted % book
    far = book + jnp.where(within // half == section_id, 0, half) + within % half
    local = jnp.where(wanted // book == slab_id, within, far)
    slot_ids = lax.broadcasted_iota(jnp.int32, (1, slots, 1), 1)
    asked = jnp.sum(jnp.where(rank[:, None, :] == slot_ids, local[:, None, :], 0), axis=-1)
    picks = (
        asked.reshape(-1, 1) == lax.broadcasted_iota(jnp.int32, (1, 2 * book), 1)
    ).astype(BF16)
    table, turned = lax.optimization_barrier((table, turned))
    words = jnp.dot(picks, table, preferred_element_type=F32).astype(BF16)
    looked = exchange(words.reshape(planes, slots, channels), PLANE)
    looked = looked.reshape(planes * slots, channels)

    own_wanted = lax.dynamic_index_in_dim(shifted, slab_id + section_id, 0, keepdims=False)
    own_holder = lax.dynamic_index_in_dim(holder, slab_id + section_id, 0, keepdims=False)
    from_each = own_holder[None, :] == lax.broadcasted_iota(jnp.int32, (planes, 1), 0)
    order = jnp.dot(from_each.astype(BF16), before, preferred_element_type=F32).astype(jnp.int32)
    order = jnp.sum(jnp.where(from_each, order, 0), axis=0)
    order = jnp.where(own_wanted >= 0, own_holder * slots + order, -1)
    gather = (
        order[:, None] == lax.broadcasted_iota(jnp.int32, (1, planes * slots), 1)
    ).astype(BF16)
    pair = jnp.dot(gather, looked, preferred_element_type=F32).astype(BF16)
    return pair, turned


def front(own_field, codebook, codes, whole):
    section_id = lax.axis_index("section")
    slab_id = lax.axis_index(SLAB)
    slabs = lax.axis_size(SLAB)
    planes = lax.axis_size(PLANE)
    row_count, batch_count, frame_count, across, channels = own_field.shape
    book = codebook.shape[0]
    positions = row_count * batch_count * frame_count * across
    mean = positions // planes
    slots = int(mean + 6 * math.sqrt(mean) + 15) // 16 * 16
    cells = (frame_count, row_count, batch_count * across, channels)

    spot = lax.broadcasted_iota(jnp.int32, (positions, 1), 0)
    share = positions // slabs
    target, spot = spot // share, spot % share
    frame, spot = spot // (share // frame_count), spot % (share // frame_count)
    row, spot = spot // (batch_count * row_count), spot % (batch_count * row_count)
    batch, column = spot // row_count, spot % row_count
    spot = (column * batch_count + batch) * frame_count + frame
    spot = spot * across + target * row_count + row
    cut = (spot == lax.broadcasted_iota(jnp.int32, (1, positions), 1)).astype(BF16)
    turned = jnp.dot(
        cut, own_field.reshape(positions, channels), preferred_element_type=F32
    ).astype(BF16)
    turned = turned.reshape(slabs, share, channels)
    turned = exchange(turned, SLAB).reshape(positions, channels)

    own = jnp.transpose(own_field, (2, 0, 1, 3, 4)).reshape(cells)

    edge = jnp.full((1,) + codes.shape[1:], -1, codes.dtype)
    shifted = jnp.concatenate([edge, codes, edge], axis=0)
    shifted = shifted.reshape(slabs + 1, row_count, batch_count, frame_count, across)
    shifted = jnp.transpose(shifted, (0, 3, 1, 2, 4)).reshape(slabs + 1, positions)
    holder = jnp.where(shifted >= 0, shifted // book % planes, -1)

    if whole:
        wanted = lax.dynamic_index_in_dim(shifted, slab_id + section_id, 0, keepdims=False)
        every = lax.all_gather(codebook, SLAB, axis=0, tiled=True)
        taken = jnp.take(every, jnp.maximum(wanted, 0), axis=0)
        pair = jnp.where(wanted[:, None] >= 0, taken, 0).astype(BF16)
    else:
        pair, turned = routed(codebook, shifted, holder, slots, turned)

    place = lax.broadcasted_iota(jnp.int32, (positions, 1), 0)
    group, column = place // across, place % across
    place = (column // row_count) * (positions // slabs) + group * row_count + column % row_count
    sent = (place == lax.broadcasted_iota(jnp.int32, (1, positions), 1)).astype(BF16)
    cotangent = jnp.dot(sent, turned, preferred_element_type=F32).astype(BF16)

    counts = jnp.sum(
        (holder[:, None, :] == lax.broadcasted_iota(jnp.int32, (1, planes, 1), 1)).astype(F32), axis=-1
    )
    crowded = (jnp.max(counts) > slots).astype(F32).reshape(1)

    other = lax.ppermute(pair, "section", [(0, 1), (1, 0)])
    return (
        pair.reshape(cells),
        other.reshape(cells),
        cotangent.reshape(frame_count, -1, channels),
        own,
        crowded,
    )


def line_shares(fields, kernels, codebook, codes, whole):
    section = lax.axis_index("section").reshape(1).astype(jnp.int32)
    slabs = lax.axis_size(SLAB)
    own_field = fields[0]
    kernel = kernels[0]
    row_count, batch_count, frame_count, across, channels = own_field.shape
    pair, other, cotangent, own, crowded = front(own_field, codebook, codes, whole)
    source = shift_source(section, pair, other, across)
    cells = decoder_grad(section, source, kernel, cotangent, own)
    above, below = neighbours(cells[:, -1], cells[:, 0], own[:, -1], own[:, 0])
    back_dec, pre_act = back_and_forth(section, cells, above, below, kernel, across)
    source = turn_source(section, source, cells, above, below, across)
    returned = lax.ppermute(back_dec, "section", [(1, 0)])

    total = (
        row_count * slabs * across * batch_count * lax.axis_size("dp") * frame_count
    )
    packed = kernel_grads(
        section, source, pre_act, cells, returned, pair, other, lax.axis_size(PLANE)
    )
    plane = exchange(packed, PLANE)
    line = exchange(sum_plane(crowded, plane, lax.axis_size(Z)), Z)
    mark = jnp.max(line[:, -8])
    return exchange(sum_line(line, 1.0 / math.sqrt(total)), Z), mark


def on_device(fields, kernels, codebook, codes):
    line, mark = line_shares(fields, kernels, codebook, codes, False)
    line = lax.cond(
        mark > 0,
        lambda frames, *args: line_shares(*args, True)[0],
        lambda frames, *args: frames,
        line,
        fields,
        kernels,
        codebook,
        codes,
    )
    planes = lax.axis_size(PLANE)
    plane = exchange(spread(line, planes), PLANE)
    return unpack(plane, kernels.shape[-1])[None]


def solution(mesh):
    sections, slabs, dps = (mesh.shape[a] for a in ("section", "slab", "dp"))
    nx = 4 if slabs >= 16 else 2
    inner = Mesh(
        mesh.devices.reshape(sections, slabs // (nx * nx), nx, nx, dps),
        ("section", "zh", "y", "x", "dp"),
    )
    placed = (
        P("section", SLAB, "dp", None, None, None),
        P("section", None, None, None, None, None),
        P(SLAB, None),
        P(None, "dp", None, None),
    )
    return jax.shard_map(
        on_device,
        mesh=inner,
        in_specs=placed,
        out_specs=P("section", None, None, None, None, None),
        check_vma=False,
    )
```

```python
import math

import jax
import jax.numpy as jnp
from jax import lax
from jax.experimental import pallas as pl
from jax.experimental.pallas import tpu as pltpu
from jax.sharding import Mesh, PartitionSpec as P

COMMIT = 0.5
SLAB = ("zh", "y", "x")
PLANE = ("y", "x")
Z = ("zh", "dp")
F32 = jnp.float32
BF16 = jnp.bfloat16
I16 = jnp.int16
TINY = 2.0**-100
STEPS = 32000.0
VMEM_LIMIT = 24 * 1024 * 1024


def silu_slope(pre_act):
    sig = jax.nn.sigmoid(pre_act)
    return sig * (1.0 + pre_act * (1.0 - sig))


def halo_pairs():
    slabs = lax.axis_size(SLAB)
    cut = slabs // lax.axis_size("zh")
    early = [(i, i + 1) for i in range(cut - 1, slabs - 1, cut)]
    late = [(i, i + 1) for i in range(2 * slabs - 1) if i != slabs - 1 and (i, i + 1) not in early]
    return late, early


def neighbours(cells, pairs):
    axes = ("section",) + SLAB
    above = lax.ppermute(cells[:, -1], axes, pairs)
    below = lax.ppermute(cells[:, 0], axes, [(j, i) for i, j in pairs])
    return above, below


def exchange(cells, axes):
    return lax.all_to_all(cells, axes, split_axis=0, concat_axis=0, tiled=True)


def coded(values):
    top = jnp.max(jnp.abs(values), axis=tuple(range(values.ndim)), keepdims=True)
    exponent = jnp.ceil(jnp.log2(top + TINY))
    return jnp.round(values * (jnp.exp2(-exponent) * STEPS)), exponent


def decoded_scale(exponents):
    return jnp.exp2(exponents.astype(F32)) * (1.0 / STEPS)


def framed(piece, mark):
    steps, exponent = coded(piece)
    row = lax.broadcasted_iota(jnp.int32, (8, 128), 0)
    tail = jnp.where(row == 0, mark, exponent)
    return jnp.concatenate([steps, tail], axis=0).astype(I16)


def unframed(wide):
    return wide[:-8] * (jnp.exp2(wide[-1:]) * (1.0 / STEPS))


def shifted_columns(block, across, tap):
    if tap == 1:
        return block
    count = block.shape[0]
    wide = block.astype(F32)
    column = lax.broadcasted_iota(jnp.int32, block.shape, 0) % across
    if tap == 0:
        wide = jnp.where(column == 0, 0.0, pltpu.roll(wide, 1, 0))
    else:
        wide = jnp.where(column == across - 1, 0.0, pltpu.roll(wide, count - 1, 0))
    return wide.astype(block.dtype)


def call(body, outs, *args, flops=0, scratch=()):
    size = sum(math.prod(a.shape) * a.dtype.itemsize for a in args) + sum(
        math.prod(o.shape) * o.dtype.itemsize for o in outs
    )
    return pl.pallas_call(
        body,
        in_specs=[pl.BlockSpec(memory_space=pltpu.SMEM)]
        + [pl.BlockSpec(memory_space=pltpu.VMEM)] * (len(args) - 1),
        out_specs=[pl.BlockSpec(memory_space=pltpu.VMEM)] * len(outs),
        out_shape=list(outs),
        scratch_shapes=list(scratch),
        cost_estimate=pl.CostEstimate(flops=flops, bytes_accessed=size, transcendentals=0),
        compiler_params=pltpu.CompilerParams(vmem_limit_bytes=VMEM_LIMIT),
    )(*args)


def shift_source(section, pair, other, across):
    frames, rows, count, channels = pair.shape

    def body(section_ref, pair_ref, other_ref, out_ref):
        @pl.when(section_ref[0] == 1)
        def _():
            for frame in range(frames):
                for row in range(rows):
                    for tap in range(3):
                        block = shifted_columns(other_ref[frame, row], across, tap)
                        out_ref[tap, frame, row] = block
                        block = shifted_columns(pair_ref[frame, row], across, tap)
                        out_ref[tap, frame, rows + row] = block

    out = jax.ShapeDtypeStruct((3, frames, 2 * rows, count, channels), BF16)
    return call(body, [out], section, pair, other)[0]


def rimmed_block(frame, row, cells_ref, above_refs, below_refs):
    rows = cells_ref.shape[1]
    if 0 < row <= rows:
        return cells_ref[frame, row - 1]
    late, early = below_refs if row else above_refs
    return late[frame] + early[frame]


def turn_source(section, source, cells, above, below, across):
    taps, frames, rows, count, channels = source.shape

    def body(section_ref, source_ref, cells_ref, *refs):
        above_refs, below_refs, out_ref = refs[:2], refs[2:4], refs[4]

        def write(block_of):
            for frame in range(frames):
                for row in range(rows):
                    start = (frame * rows + row) * count
                    for tap in range(taps):
                        out_ref[tap, :, start : start + count] = block_of(tap, frame, row).T

        def encoder_block(tap, frame, row):
            block = rimmed_block(frame, row, cells_ref, above_refs, below_refs)
            return shifted_columns(block, across, tap)

        @pl.when(section_ref[0] == 0)
        def _():
            write(encoder_block)

        @pl.when(section_ref[0] == 1)
        def _():
            write(lambda tap, frame, row: source_ref[tap, frame, row])

    out = jax.ShapeDtypeStruct((taps, channels, frames * rows * count), BF16)
    return call(body, [out], section, source, cells, *above, *below)[0]


def tap_index(section_ref, row_tap, column_tap):
    decoder = section_ref[0] == 1
    return jnp.where(decoder, column_tap, row_tap), jnp.where(decoder, row_tap, column_tap)


def convolved(section_ref, source_ref, kernel_ref, frame):
    _, _, rimmed, count, channels = source_ref.shape
    rows = rimmed - 2
    acc = jnp.zeros((rows * count, channels), F32)
    for r in range(3):
        for q in range(3):
            i, j = tap_index(section_ref, r, q)
            for back in range(frame + 1):
                cells = source_ref[q, frame - back, r : r + rows].reshape(rows * count, channels)
                acc += jnp.dot(cells, kernel_ref[1 - back, i, j], preferred_element_type=F32)
    return acc


def decoder_grad(section, source, kernel, cotangent, own):
    frames, rows, count, channels = own.shape

    def body(section_ref, source_ref, kernel_ref, cot_ref, own_ref, out_ref):
        @pl.when(section_ref[0] == 0)
        def _():
            out_ref[...] = own_ref[...]

        @pl.when(section_ref[0] == 1)
        def _():
            for frame in range(frames):
                slope = silu_slope(convolved(section_ref, source_ref, kernel_ref, frame))
                grad = (cot_ref[frame].astype(F32) * slope).astype(BF16)
                out_ref[frame] = grad.reshape(rows, count, channels)

    return call(
        body,
        [jax.ShapeDtypeStruct(own.shape, BF16)],
        section,
        source,
        kernel,
        cotangent,
        own,
        flops=54 * rows * count * channels * channels,
    )[0]


def back_and_forth(section, cells, above, below, kernel, across):
    frames, rows, count, channels = cells.shape
    span = rows * count

    def body(section_ref, cells_ref, *refs):
        above_refs, below_refs = refs[:2], refs[2:4]
        kernel_ref, back_ref, pre_ref, shifted = refs[4:]
        for frame in range(frames):
            for row in range(rows + 2):
                block = rimmed_block(frame, row, cells_ref, above_refs, below_refs)
                for tap in range(3):
                    shifted[tap, frame, row] = shifted_columns(block, across, tap)

        @pl.when(section_ref[0] == 0)
        def _():
            for frame in range(frames):
                pre_ref[frame] = convolved(section_ref, shifted, kernel_ref, frame)

        @pl.when(section_ref[0] == 1)
        def _():
            for frame in range(frames):
                acc = jnp.zeros((span, channels), F32)
                for r in range(3):
                    for q in range(3):
                        i, j = tap_index(section_ref, r, q)
                        for ahead in range(frames - frame):
                            grads = shifted[2 - q, frame + ahead, 2 - r : 2 - r + rows]
                            acc += lax.dot_general(
                                grads.reshape(span, channels),
                                kernel_ref[1 - ahead, i, j],
                                (((1,), (1,)), ((), ())),
                                preferred_element_type=F32,
                            )
                back_ref[frame] = acc.astype(BF16).reshape(rows, count, channels)

    return call(
        body,
        [
            jax.ShapeDtypeStruct(cells.shape, BF16),
            jax.ShapeDtypeStruct((frames, span, channels), F32),
        ],
        section,
        cells,
        *above,
        *below,
        kernel,
        flops=54 * span * channels * channels,
        scratch=[pltpu.VMEM((3, frames, rows + 2, count, channels), BF16)],
    )


def kernel_grads(section, turned, pre_act, dec_grad, returned, pair, other, parts):
    _, channels, _ = turned.shape
    frames, rows, count, _ = returned.shape
    span = rows * count
    size = channels // parts

    def body(
        section_ref, turned_ref, pre_ref, dec_ref, returned_ref, pair_ref, other_ref,
        out_ref, side, grads,
    ):
        @pl.when(section_ref[0] == 0)
        def _():
            for frame in range(frames):
                for row, quant in enumerate((pair_ref[frame, 1], other_ref[frame, 0])):
                    at = slice(row * count, (row + 1) * count)
                    side[frame, at] = (
                        returned_ref[frame, row].astype(F32)
                        + COMMIT * (pre_ref[frame, at] - quant.astype(F32))
                    ).astype(BF16)

        @pl.when(section_ref[0] == 1)
        def _():
            side[...] = dec_ref[...].reshape(frames, span, channels)

        top = jnp.zeros((8, channels), F32)
        for r in range(3):
            for q in range(3):
                i, j = tap_index(section_ref, r, q)
                tap = i * 3 + j
                first = turned_ref[q, :, r * count : r * count + span]
                start = (rows + 2 + r) * count
                second = turned_ref[q, :, start : start + span]
                late = jnp.dot(first, side[1], preferred_element_type=F32)
                same = jnp.dot(first, side[0], preferred_element_type=F32)
                same += jnp.dot(second, side[1], preferred_element_type=F32)
                for at, values in ((tap, late), (9 + tap, same)):
                    grads[at] = values
                    seen = jnp.max(jnp.abs(values).reshape(-1, 8, channels), axis=0)
                    top = jnp.maximum(top, seen)
        exponent = jnp.ceil(jnp.log2(jnp.max(top, axis=(0, 1), keepdims=True) + TINY))
        factor = jnp.exp2(-exponent) * STEPS

        @pl.loop(0, 18)
        def _(tap):
            steps = jnp.round(grads[tap] * factor).astype(I16)
            out_ref[:, tap] = steps.reshape(parts, size, channels)

        tail = jnp.broadcast_to(exponent, (size, channels)).astype(I16)
        for part in range(parts):
            out_ref[part, 18] = tail

    return call(
        body,
        [jax.ShapeDtypeStruct((parts, 19, size, channels), I16)],
        section,
        turned,
        pre_act,
        dec_grad,
        returned,
        pair,
        other,
        flops=54 * span * channels * channels,
        scratch=[
            pltpu.VMEM((frames, span, channels), BF16),
            pltpu.VMEM((18, channels, channels), F32),
        ],
    )[0]


def sum_plane(crowded, packed, pieces):
    senders, taps, size, outs = packed.shape
    taps = taps - 1
    half = taps // 2

    def body(crowded_ref, packed_ref, framed_ref, total):
        mark = jnp.full((1, 128), crowded_ref[0])
        scales = [decoded_scale(packed_ref[s, taps])[:1, :1] for s in range(senders)]
        for tap in range(taps):
            acc = packed_ref[0, tap].astype(F32) * scales[0]
            for s in range(1, senders):
                acc += packed_ref[s, tap].astype(F32) * scales[s]
            total[tap] = acc
        place = 0
        for frame in range(2):
            for oct_ in range(size // 8):
                for lane in range(outs // 128):
                    piece = total[
                        frame * half : (frame + 1) * half,
                        oct_ * 8 : oct_ * 8 + 8,
                        lane * 128 : lane * 128 + 128,
                    ]
                    framed_ref[place] = framed(piece.reshape(half * 8, 128), mark)
                    place += 1

    return pl.pallas_call(
        body,
        in_specs=[
            pl.BlockSpec(memory_space=pltpu.SMEM),
            pl.BlockSpec(memory_space=pltpu.VMEM),
        ],
        out_shape=jax.ShapeDtypeStruct((pieces, half * 8 + 8, 128), I16),
        scratch_shapes=[pltpu.VMEM((taps, size, outs), F32)],
        compiler_params=pltpu.CompilerParams(vmem_limit_bytes=VMEM_LIMIT),
    )(crowded, packed)


def sum_line(framed_parts, factor):
    def body(parts_ref, out_ref):
        first = parts_ref[0].astype(F32)
        acc, mark = unframed(first), first[-8:-7]
        for s in range(1, framed_parts.shape[0]):
            part = parts_ref[s].astype(F32)
            acc += unframed(part)
            mark = jnp.maximum(mark, part[-8:-7])
        result = framed(acc * factor, mark)
        for s in range(framed_parts.shape[0]):
            out_ref[s] = result

    return pl.pallas_call(
        body, out_shape=jax.ShapeDtypeStruct(framed_parts.shape, I16)
    )(framed_parts)


def spread(line, parts):
    pieces, rows, _ = line.shape
    rows -= 8

    def body(line_ref, out_ref):
        wide = [line_ref[p].astype(F32) for p in range(pieces)]
        row = lax.broadcasted_iota(jnp.int32, (16, 128), 0)
        tail = jnp.zeros((16, 128), F32)
        for p in range(pieces):
            tail = jnp.where(row == p, wide[p][-1:], tail)
        result = jnp.concatenate([w[:-8] for w in wide] + [tail], axis=0).astype(I16)
        for part in range(parts):
            out_ref[part] = result

    return pl.pallas_call(
        body, out_shape=jax.ShapeDtypeStruct((parts, pieces * rows + 16, 128), I16)
    )(line)


def unpack(plane, channels):
    parts, rows, _ = plane.shape
    size = channels // parts
    pieces = 2 * (size // 8) * (channels // 128)
    each = (rows - 16) // pieces
    group = 4

    def body(plane_ref, out_ref):
        for part in range(group):
            wide = plane_ref[part].astype(F32)
            scales = jnp.exp2(wide[-16:]) * (1.0 / STEPS)
            place = 0
            for frame in range(2):
                for oct_ in range(size // 8):
                    for lane in range(channels // 128):
                        piece = wide[place * each : (place + 1) * each] * scales[place : place + 1]
                        row = part * size + oct_ * 8
                        out_ref[
                            frame, :, :, row : row + 8, lane * 128 : lane * 128 + 128
                        ] = piece.reshape(3, 3, 8, 128)
                        place += 1

    return pl.pallas_call(
        body,
        grid=(parts // group,),
        in_specs=[pl.BlockSpec((group, rows, 128), lambda k: (k, 0, 0))],
        out_specs=pl.BlockSpec((2, 3, 3, group * size, channels), lambda k: (0, 0, 0, k, 0)),
        out_shape=jax.ShapeDtypeStruct((2, 3, 3, channels, channels), F32),
        compiler_params=pltpu.CompilerParams(vmem_limit_bytes=VMEM_LIMIT),
    )(plane)


def routed(codebook, shifted, holder, slots, turned, early):
    section_id = lax.axis_index("section")
    slab_id = lax.axis_index(SLAB)
    near = lax.axis_index("zh")
    plane_id = lax.axis_index(PLANE)
    planes = lax.axis_size(PLANE)
    book, channels = codebook.shape
    positions = shifted.shape[1]

    half = book // 2
    got = lax.ppermute(
        lax.dynamic_slice_in_dim(codebook, section_id * half, half, 0), "zh", [(0, 1), (1, 0)]
    )
    table = jnp.concatenate(
        [codebook, got, lax.ppermute(got, "section", [(0, 1), (1, 0)])], axis=0
    )

    before = (
        lax.broadcasted_iota(jnp.int32, (positions, positions), 0)
        < lax.broadcasted_iota(jnp.int32, (positions, positions), 1)
    ).astype(BF16)

    start = near * planes + section_id
    wanted = lax.dynamic_slice_in_dim(shifted, start, planes, 0)
    mine = lax.dynamic_slice_in_dim(holder, start, planes, 0) == plane_id
    rank = jnp.dot(mine.astype(BF16), before, preferred_element_type=F32).astype(jnp.int32)
    rank = jnp.where(mine, rank, -1)
    within = wanted % book
    far = book + jnp.where(within // half == section_id, 0, half) + within % half
    local = jnp.where(wanted // book == slab_id, within, far)
    slot_ids = lax.broadcasted_iota(jnp.int32, (1, slots, 1), 1)
    asked = jnp.sum(jnp.where(rank[:, None, :] == slot_ids, local[:, None, :], 0), axis=-1)
    picks = (
        asked.reshape(-1, 1) == lax.broadcasted_iota(jnp.int32, (1, 2 * book), 1)
    ).astype(BF16)
    table, turned = lax.optimization_barrier((table, turned))
    words = jnp.dot(picks, table, preferred_element_type=F32).astype(BF16)
    looked = exchange(words.reshape(planes, slots, channels), PLANE)
    looked = looked.reshape(planes * slots, channels)
    looked, early = lax.optimization_barrier((looked, early))

    own_wanted = lax.dynamic_index_in_dim(shifted, slab_id + section_id, 0, keepdims=False)
    own_holder = lax.dynamic_index_in_dim(holder, slab_id + section_id, 0, keepdims=False)
    from_each = own_holder[None, :] == lax.broadcasted_iota(jnp.int32, (planes, 1), 0)
    order = jnp.dot(from_each.astype(BF16), before, preferred_element_type=F32).astype(jnp.int32)
    order = jnp.sum(jnp.where(from_each, order, 0), axis=0)
    order = jnp.where(own_wanted >= 0, own_holder * slots + order, -1)
    gather = (
        order[:, None] == lax.broadcasted_iota(jnp.int32, (1, planes * slots), 1)
    ).astype(BF16)
    pair = jnp.dot(gather, looked, preferred_element_type=F32).astype(BF16)
    return pair, turned, early


def front(own_field, codebook, codes, whole):
    section_id = lax.axis_index("section")
    slab_id = lax.axis_index(SLAB)
    slabs = lax.axis_size(SLAB)
    planes = lax.axis_size(PLANE)
    row_count, batch_count, frame_count, across, channels = own_field.shape
    book = codebook.shape[0]
    positions = row_count * batch_count * frame_count * across
    mean = positions // planes
    slots = int(mean + 6 * math.sqrt(mean) + 15) // 16 * 16
    cells = (frame_count, row_count, batch_count * across, channels)

    spot = lax.broadcasted_iota(jnp.int32, (positions, 1), 0)
    share = positions // slabs
    target, spot = spot // share, spot % share
    frame, spot = spot // (share // frame_count), spot % (share // frame_count)
    row, spot = spot // (batch_count * row_count), spot % (batch_count * row_count)
    batch, column = spot // row_count, spot % row_count
    spot = (column * batch_count + batch) * frame_count + frame
    spot = spot * across + target * row_count + row
    cut = (spot == lax.broadcasted_iota(jnp.int32, (1, positions), 1)).astype(BF16)
    turned = jnp.dot(
        cut, own_field.reshape(positions, channels), preferred_element_type=F32
    ).astype(BF16)
    turned = turned.reshape(slabs, share, channels)
    turned = exchange(turned, SLAB).reshape(positions, channels)

    own = jnp.transpose(own_field, (2, 0, 1, 3, 4)).reshape(cells)
    early = neighbours(own, halo_pairs()[1])

    edge = jnp.full((1,) + codes.shape[1:], -1, codes.dtype)
    shifted = jnp.concatenate([edge, codes, edge], axis=0)
    shifted = shifted.reshape(slabs + 1, row_count, batch_count, frame_count, across)
    shifted = jnp.transpose(shifted, (0, 3, 1, 2, 4)).reshape(slabs + 1, positions)
    holder = jnp.where(shifted >= 0, shifted // book % planes, -1)

    if whole:
        wanted = lax.dynamic_index_in_dim(shifted, slab_id + section_id, 0, keepdims=False)
        every = lax.all_gather(codebook, SLAB, axis=0, tiled=True)
        taken = jnp.take(every, jnp.maximum(wanted, 0), axis=0)
        pair = jnp.where(wanted[:, None] >= 0, taken, 0).astype(BF16)
    else:
        pair, turned, early = routed(codebook, shifted, holder, slots, turned, early)

    place = lax.broadcasted_iota(jnp.int32, (positions, 1), 0)
    group, column = place // across, place % across
    place = (column // row_count) * (positions // slabs) + group * row_count + column % row_count
    sent = (place == lax.broadcasted_iota(jnp.int32, (1, positions), 1)).astype(BF16)
    cotangent = jnp.dot(sent, turned, preferred_element_type=F32).astype(BF16)

    counts = jnp.sum(
        (holder[:, None, :] == lax.broadcasted_iota(jnp.int32, (1, planes, 1), 1)).astype(F32), axis=-1
    )
    crowded = (jnp.max(counts) > slots).astype(F32).reshape(1)

    other = lax.ppermute(pair, "section", [(0, 1), (1, 0)])
    return (
        pair.reshape(cells),
        other.reshape(cells),
        cotangent.reshape(frame_count, -1, channels),
        own,
        early,
        crowded,
    )


def line_shares(fields, kernels, codebook, codes, whole):
    section = lax.axis_index("section").reshape(1).astype(jnp.int32)
    slabs = lax.axis_size(SLAB)
    own_field = fields[0]
    kernel = kernels[0]
    row_count, batch_count, frame_count, across, channels = own_field.shape
    pair, other, cotangent, own, early, crowded = front(own_field, codebook, codes, whole)
    source = shift_source(section, pair, other, across)
    cells = decoder_grad(section, source, kernel, cotangent, own)
    above, below = zip(neighbours(cells, halo_pairs()[0]), early)
    back_dec, pre_act = back_and_forth(section, cells, above, below, kernel, across)
    source = turn_source(section, source, cells, above, below, across)
    returned = lax.ppermute(back_dec, "section", [(1, 0)])

    total = (
        row_count * slabs * across * batch_count * lax.axis_size("dp") * frame_count
    )
    packed = kernel_grads(
        section, source, pre_act, cells, returned, pair, other, lax.axis_size(PLANE)
    )
    plane = exchange(packed, PLANE)
    line = exchange(sum_plane(crowded, plane, lax.axis_size(Z)), Z)
    mark = jnp.max(line[:, -8])
    return exchange(sum_line(line, 1.0 / math.sqrt(total)), Z), mark


def on_device(fields, kernels, codebook, codes):
    line, mark = line_shares(fields, kernels, codebook, codes, False)
    line = lax.cond(
        mark > 0,
        lambda frames, *args: line_shares(*args, True)[0],
        lambda frames, *args: frames,
        line,
        fields,
        kernels,
        codebook,
        codes,
    )
    planes = lax.axis_size(PLANE)
    plane = exchange(spread(line, planes), PLANE)
    return unpack(plane, kernels.shape[-1])[None]


def solution(mesh):
    sections, slabs, dps = (mesh.shape[a] for a in ("section", "slab", "dp"))
    nx = 4 if slabs >= 16 else 2
    inner = Mesh(
        mesh.devices.reshape(sections, slabs // (nx * nx), nx, nx, dps),
        ("section", "zh", "y", "x", "dp"),
    )
    placed = (
        P("section", SLAB, "dp", None, None, None),
        P("section", None, None, None, None, None),
        P(SLAB, None),
        P(None, "dp", None, None),
    )
    return jax.shard_map(
        on_device,
        mesh=inner,
        in_specs=placed,
        out_specs=P("section", None, None, None, None, None),
        check_vma=False,
    )
```

```python
import math

import jax
import jax.numpy as jnp
from jax import lax
from jax.experimental import pallas as pl
from jax.experimental.pallas import tpu as pltpu
from jax.sharding import Mesh, PartitionSpec as P

COMMIT = 0.5
SLAB = ("zh", "y", "x")
PLANE = ("y", "x")
Z = ("zh", "dp")
F32 = jnp.float32
BF16 = jnp.bfloat16
I16 = jnp.int16
TINY = 2.0**-100
STEPS = 32000.0
VMEM_LIMIT = 24 * 1024 * 1024


def silu_slope(pre_act):
    sig = jax.nn.sigmoid(pre_act)
    return sig * (1.0 + pre_act * (1.0 - sig))


def neighbours(lower, upper):
    count = lax.axis_size(SLAB)
    above = lax.ppermute(lower, SLAB, [(i, i + 1) for i in range(count - 1)])
    below = lax.ppermute(upper, SLAB, [(i + 1, i) for i in range(count - 1)])
    none = jnp.zeros_like(lower)
    return (above, none), (below, none)


def exchange(cells, axes):
    return lax.all_to_all(cells, axes, split_axis=0, concat_axis=0, tiled=True)


def coded(values):
    top = jnp.max(jnp.abs(values), axis=tuple(range(values.ndim)), keepdims=True)
    exponent = jnp.ceil(jnp.log2(top + TINY))
    return jnp.round(values * (jnp.exp2(-exponent) * STEPS)), exponent


def decoded_scale(exponents):
    return jnp.exp2(exponents.astype(F32)) * (1.0 / STEPS)


def framed(piece, mark):
    steps, exponent = coded(piece)
    row = lax.broadcasted_iota(jnp.int32, (8, 128), 0)
    tail = jnp.where(row == 0, mark, exponent)
    return jnp.concatenate([steps, tail], axis=0).astype(I16)


def unframed(wide):
    return wide[:-8] * (jnp.exp2(wide[-1:]) * (1.0 / STEPS))


def shifted_columns(block, across, tap):
    if tap == 1:
        return block
    count = block.shape[0]
    wide = block.astype(F32)
    column = lax.broadcasted_iota(jnp.int32, block.shape, 0) % across
    if tap == 0:
        wide = jnp.where(column == 0, 0.0, pltpu.roll(wide, 1, 0))
    else:
        wide = jnp.where(column == across - 1, 0.0, pltpu.roll(wide, count - 1, 0))
    return wide.astype(block.dtype)


def call(body, outs, *args, flops=0, scratch=()):
    size = sum(math.prod(a.shape) * a.dtype.itemsize for a in args) + sum(
        math.prod(o.shape) * o.dtype.itemsize for o in outs
    )
    return pl.pallas_call(
        body,
        in_specs=[pl.BlockSpec(memory_space=pltpu.SMEM)]
        + [pl.BlockSpec(memory_space=pltpu.VMEM)] * (len(args) - 1),
        out_specs=[pl.BlockSpec(memory_space=pltpu.VMEM)] * len(outs),
        out_shape=list(outs),
        scratch_shapes=list(scratch),
        cost_estimate=pl.CostEstimate(flops=flops, bytes_accessed=size, transcendentals=0),
        compiler_params=pltpu.CompilerParams(vmem_limit_bytes=VMEM_LIMIT),
    )(*args)


def shift_source(section, pair, other, across):
    frames, rows, count, channels = pair.shape

    def body(section_ref, pair_ref, other_ref, out_ref):
        @pl.when(section_ref[0] == 1)
        def _():
            for frame in range(frames):
                for row in range(rows):
                    for tap in range(3):
                        block = shifted_columns(other_ref[frame, row], across, tap)
                        out_ref[tap, frame, row] = block
                        block = shifted_columns(pair_ref[frame, row], across, tap)
                        out_ref[tap, frame, rows + row] = block

    out = jax.ShapeDtypeStruct((3, frames, 2 * rows, count, channels), BF16)
    return call(body, [out], section, pair, other)[0]


def rimmed_block(frame, row, cells_ref, above_refs, below_refs):
    rows = cells_ref.shape[1]
    if 0 < row <= rows:
        return cells_ref[frame, row - 1]
    late, early = below_refs if row else above_refs
    return late[frame] + early[frame]


def turn_source(section, source, cells, above, below, across):
    taps, frames, rows, count, channels = source.shape

    def body(section_ref, source_ref, cells_ref, *refs):
        above_refs, below_refs, out_ref = refs[:2], refs[2:4], refs[4]

        def write(block_of):
            for frame in range(frames):
                for row in range(rows):
                    start = (frame * rows + row) * count
                    for tap in range(taps):
                        out_ref[tap, :, start : start + count] = block_of(tap, frame, row).T

        def encoder_block(tap, frame, row):
            block = rimmed_block(frame, row, cells_ref, above_refs, below_refs)
            return shifted_columns(block, across, tap)

        @pl.when(section_ref[0] == 0)
        def _():
            write(encoder_block)

        @pl.when(section_ref[0] == 1)
        def _():
            write(lambda tap, frame, row: source_ref[tap, frame, row])

    out = jax.ShapeDtypeStruct((taps, channels, frames * rows * count), BF16)
    return call(body, [out], section, source, cells, *above, *below)[0]


def tap_index(section_ref, row_tap, column_tap):
    decoder = section_ref[0] == 1
    return jnp.where(decoder, column_tap, row_tap), jnp.where(decoder, row_tap, column_tap)


def convolved(section_ref, source_ref, kernel_ref, frame):
    _, _, rimmed, count, channels = source_ref.shape
    rows = rimmed - 2
    acc = jnp.zeros((rows * count, channels), F32)
    for r in range(3):
        for q in range(3):
            i, j = tap_index(section_ref, r, q)
            for back in range(frame + 1):
                cells = source_ref[q, frame - back, r : r + rows].reshape(rows * count, channels)
                acc += jnp.dot(cells, kernel_ref[1 - back, i, j], preferred_element_type=F32)
    return acc


def decoder_grad(section, source, kernel, cotangent, own):
    frames, rows, count, channels = own.shape

    def body(section_ref, source_ref, kernel_ref, cot_ref, own_ref, out_ref):
        @pl.when(section_ref[0] == 0)
        def _():
            out_ref[...] = own_ref[...]

        @pl.when(section_ref[0] == 1)
        def _():
            for frame in range(frames):
                slope = silu_slope(convolved(section_ref, source_ref, kernel_ref, frame))
                grad = (cot_ref[frame].astype(F32) * slope).astype(BF16)
                out_ref[frame] = grad.reshape(rows, count, channels)

    return call(
        body,
        [jax.ShapeDtypeStruct(own.shape, BF16)],
        section,
        source,
        kernel,
        cotangent,
        own,
        flops=54 * rows * count * channels * channels,
    )[0]


def back_and_forth(section, cells, above, below, kernel, across):
    frames, rows, count, channels = cells.shape
    span = rows * count

    def body(section_ref, cells_ref, *refs):
        above_refs, below_refs = refs[:2], refs[2:4]
        kernel_ref, back_ref, pre_ref, shifted = refs[4:]
        for frame in range(frames):
            for row in range(rows + 2):
                block = rimmed_block(frame, row, cells_ref, above_refs, below_refs)
                for tap in range(3):
                    shifted[tap, frame, row] = shifted_columns(block, across, tap)

        @pl.when(section_ref[0] == 0)
        def _():
            for frame in range(frames):
                pre_ref[frame] = convolved(section_ref, shifted, kernel_ref, frame)

        @pl.when(section_ref[0] == 1)
        def _():
            for frame in range(frames):
                acc = jnp.zeros((span, channels), F32)
                for r in range(3):
                    for q in range(3):
                        i, j = tap_index(section_ref, r, q)
                        for ahead in range(frames - frame):
                            grads = shifted[2 - q, frame + ahead, 2 - r : 2 - r + rows]
                            acc += lax.dot_general(
                                grads.reshape(span, channels),
                                kernel_ref[1 - ahead, i, j],
                                (((1,), (1,)), ((), ())),
                                preferred_element_type=F32,
                            )
                back_ref[frame] = acc.astype(BF16).reshape(rows, count, channels)

    return call(
        body,
        [
            jax.ShapeDtypeStruct(cells.shape, BF16),
            jax.ShapeDtypeStruct((frames, span, channels), F32),
        ],
        section,
        cells,
        *above,
        *below,
        kernel,
        flops=54 * span * channels * channels,
        scratch=[pltpu.VMEM((3, frames, rows + 2, count, channels), BF16)],
    )


def kernel_grads(section, turned, pre_act, dec_grad, returned, pair, other, parts):
    _, channels, _ = turned.shape
    frames, rows, count, _ = returned.shape
    span = rows * count
    size = channels // parts

    def body(
        section_ref, turned_ref, pre_ref, dec_ref, returned_ref, pair_ref, other_ref,
        out_ref, side, grads,
    ):
        @pl.when(section_ref[0] == 0)
        def _():
            for frame in range(frames):
                for row, quant in enumerate((pair_ref[frame, 1], other_ref[frame, 0])):
                    at = slice(row * count, (row + 1) * count)
                    side[frame, at] = (
                        returned_ref[frame, row].astype(F32)
                        + COMMIT * (pre_ref[frame, at] - quant.astype(F32))
                    ).astype(BF16)

        @pl.when(section_ref[0] == 1)
        def _():
            side[...] = dec_ref[...].reshape(frames, span, channels)

        top = jnp.zeros((8, channels), F32)
        for r in range(3):
            for q in range(3):
                i, j = tap_index(section_ref, r, q)
                tap = i * 3 + j
                first = turned_ref[q, :, r * count : r * count + span]
                start = (rows + 2 + r) * count
                second = turned_ref[q, :, start : start + span]
                late = jnp.dot(first, side[1], preferred_element_type=F32)
                same = jnp.dot(first, side[0], preferred_element_type=F32)
                same += jnp.dot(second, side[1], preferred_element_type=F32)
                for at, values in ((tap, late), (9 + tap, same)):
                    grads[at] = values
                    seen = jnp.max(jnp.abs(values).reshape(-1, 8, channels), axis=0)
                    top = jnp.maximum(top, seen)
        exponent = jnp.ceil(jnp.log2(jnp.max(top, axis=(0, 1), keepdims=True) + TINY))
        factor = jnp.exp2(-exponent) * STEPS

        @pl.loop(0, 18)
        def _(tap):
            steps = jnp.round(grads[tap] * factor).astype(I16)
            out_ref[:, tap] = steps.reshape(parts, size, channels)

        tail = jnp.broadcast_to(exponent, (size, channels)).astype(I16)
        for part in range(parts):
            out_ref[part, 18] = tail

    return call(
        body,
        [jax.ShapeDtypeStruct((parts, 19, size, channels), I16)],
        section,
        turned,
        pre_act,
        dec_grad,
        returned,
        pair,
        other,
        flops=54 * span * channels * channels,
        scratch=[
            pltpu.VMEM((frames, span, channels), BF16),
            pltpu.VMEM((18, channels, channels), F32),
        ],
    )[0]


def sum_plane(crowded, packed, pieces):
    senders, taps, size, outs = packed.shape
    taps = taps - 1
    half = taps // 2

    def body(crowded_ref, packed_ref, framed_ref, total):
        mark = jnp.full((1, 128), crowded_ref[0])
        scales = [decoded_scale(packed_ref[s, taps])[:1, :1] for s in range(senders)]
        for tap in range(taps):
            acc = packed_ref[0, tap].astype(F32) * scales[0]
            for s in range(1, senders):
                acc += packed_ref[s, tap].astype(F32) * scales[s]
            total[tap] = acc
        place = 0
        for frame in range(2):
            for oct_ in range(size // 8):
                for lane in range(outs // 128):
                    piece = total[
                        frame * half : (frame + 1) * half,
                        oct_ * 8 : oct_ * 8 + 8,
                        lane * 128 : lane * 128 + 128,
                    ]
                    framed_ref[place] = framed(piece.reshape(half * 8, 128), mark)
                    place += 1

    return pl.pallas_call(
        body,
        in_specs=[
            pl.BlockSpec(memory_space=pltpu.SMEM),
            pl.BlockSpec(memory_space=pltpu.VMEM),
        ],
        out_shape=jax.ShapeDtypeStruct((pieces, half * 8 + 8, 128), I16),
        scratch_shapes=[pltpu.VMEM((taps, size, outs), F32)],
        compiler_params=pltpu.CompilerParams(vmem_limit_bytes=VMEM_LIMIT),
    )(crowded, packed)


def sum_line(framed_parts, factor):
    def body(parts_ref, out_ref):
        first = parts_ref[0].astype(F32)
        acc, mark = unframed(first), first[-8:-7]
        for s in range(1, framed_parts.shape[0]):
            part = parts_ref[s].astype(F32)
            acc += unframed(part)
            mark = jnp.maximum(mark, part[-8:-7])
        result = framed(acc * factor, mark)
        for s in range(framed_parts.shape[0]):
            out_ref[s] = result

    return pl.pallas_call(
        body, out_shape=jax.ShapeDtypeStruct(framed_parts.shape, I16)
    )(framed_parts)


def spread(line, parts):
    pieces, rows, _ = line.shape
    rows -= 8

    def body(line_ref, out_ref):
        wide = [line_ref[p].astype(F32) for p in range(pieces)]
        row = lax.broadcasted_iota(jnp.int32, (16, 128), 0)
        tail = jnp.zeros((16, 128), F32)
        for p in range(pieces):
            tail = jnp.where(row == p, wide[p][-1:], tail)
        result = jnp.concatenate([w[:-8] for w in wide] + [tail], axis=0).astype(I16)
        for part in range(parts):
            out_ref[part] = result

    return pl.pallas_call(
        body, out_shape=jax.ShapeDtypeStruct((parts, pieces * rows + 16, 128), I16)
    )(line)


def unpack(plane, channels):
    parts, rows, _ = plane.shape
    size = channels // parts
    pieces = 2 * (size // 8) * (channels // 128)
    each = (rows - 16) // pieces
    group = 4

    def body(plane_ref, out_ref):
        for part in range(group):
            wide = plane_ref[part].astype(F32)
            scales = jnp.exp2(wide[-16:]) * (1.0 / STEPS)
            place = 0
            for frame in range(2):
                for oct_ in range(size // 8):
                    for lane in range(channels // 128):
                        piece = wide[place * each : (place + 1) * each] * scales[place : place + 1]
                        row = part * size + oct_ * 8
                        out_ref[
                            frame, :, :, row : row + 8, lane * 128 : lane * 128 + 128
                        ] = piece.reshape(3, 3, 8, 128)
                        place += 1

    return pl.pallas_call(
        body,
        grid=(parts // group,),
        in_specs=[pl.BlockSpec((group, rows, 128), lambda k: (k, 0, 0))],
        out_specs=pl.BlockSpec((2, 3, 3, group * size, channels), lambda k: (0, 0, 0, k, 0)),
        out_shape=jax.ShapeDtypeStruct((2, 3, 3, channels, channels), F32),
        compiler_params=pltpu.CompilerParams(vmem_limit_bytes=VMEM_LIMIT),
    )(plane)


def routed(codebook, shifted, holder, slots, turned):
    section_id = lax.axis_index("section")
    slab_id = lax.axis_index(SLAB)
    near = lax.axis_index("zh")
    plane_id = lax.axis_index(PLANE)
    planes = lax.axis_size(PLANE)
    book, channels = codebook.shape
    positions = shifted.shape[1]

    half = book // 2
    got = lax.ppermute(
        lax.dynamic_slice_in_dim(codebook, section_id * half, half, 0), "zh", [(0, 1), (1, 0)]
    )
    table = jnp.concatenate(
        [codebook, got, lax.ppermute(got, "section", [(0, 1), (1, 0)])], axis=0
    )

    before = (
        lax.broadcasted_iota(jnp.int32, (positions, positions), 0)
        < lax.broadcasted_iota(jnp.int32, (positions, positions), 1)
    ).astype(BF16)

    start = near * planes + section_id
    wanted = lax.dynamic_slice_in_dim(shifted, start, planes, 0)
    mine = lax.dynamic_slice_in_dim(holder, start, planes, 0) == plane_id
    rank = jnp.dot(mine.astype(BF16), before, preferred_element_type=F32).astype(jnp.int32)
    rank = jnp.where(mine, rank, -1)
    within = wanted % book
    far = book + jnp.where(within // half == section_id, 0, half) + within % half
    local = jnp.where(wanted // book == slab_id, within, far)
    slot_ids = lax.broadcasted_iota(jnp.int32, (1, slots, 1), 1)
    asked = jnp.sum(jnp.where(rank[:, None, :] == slot_ids, local[:, None, :], 0), axis=-1)
    picks = (
        asked.reshape(-1, 1) == lax.broadcasted_iota(jnp.int32, (1, 2 * book), 1)
    ).astype(BF16)
    table, turned = lax.optimization_barrier((table, turned))
    words = jnp.dot(picks, table, preferred_element_type=F32).astype(BF16)
    looked = exchange(words.reshape(planes, slots, channels), PLANE)
    looked = looked.reshape(planes * slots, channels)

    own_wanted = lax.dynamic_index_in_dim(shifted, slab_id + section_id, 0, keepdims=False)
    own_holder = lax.dynamic_index_in_dim(holder, slab_id + section_id, 0, keepdims=False)
    from_each = own_holder[None, :] == lax.broadcasted_iota(jnp.int32, (planes, 1), 0)
    order = jnp.dot(from_each.astype(BF16), before, preferred_element_type=F32).astype(jnp.int32)
    order = jnp.sum(jnp.where(from_each, order, 0), axis=0)
    order = jnp.where(own_wanted >= 0, own_holder * slots + order, -1)
    gather = (
        order[:, None] == lax.broadcasted_iota(jnp.int32, (1, planes * slots), 1)
    ).astype(BF16)
    pair = jnp.dot(gather, looked, preferred_element_type=F32).astype(BF16)
    return pair, turned


def front(own_field, codebook, codes, whole):
    section_id = lax.axis_index("section")
    slab_id = lax.axis_index(SLAB)
    slabs = lax.axis_size(SLAB)
    planes = lax.axis_size(PLANE)
    row_count, batch_count, frame_count, across, channels = own_field.shape
    book = codebook.shape[0]
    positions = row_count * batch_count * frame_count * across
    mean = positions // planes
    slots = int(mean + 6 * math.sqrt(mean) + 15) // 16 * 16
    cells = (frame_count, row_count, batch_count * across, channels)

    spot = lax.broadcasted_iota(jnp.int32, (positions, 1), 0)
    share = positions // slabs
    target, spot = spot // share, spot % share
    frame, spot = spot // (share // frame_count), spot % (share // frame_count)
    row, spot = spot // (batch_count * row_count), spot % (batch_count * row_count)
    batch, column = spot // row_count, spot % row_count
    spot = (column * batch_count + batch) * frame_count + frame
    spot = spot * across + target * row_count + row
    cut = (spot == lax.broadcasted_iota(jnp.int32, (1, positions), 1)).astype(BF16)
    turned = jnp.dot(
        cut, own_field.reshape(positions, channels), preferred_element_type=F32
    ).astype(BF16)
    turned = turned.reshape(slabs, share, channels)
    turned = exchange(turned, SLAB).reshape(positions, channels)

    own = jnp.transpose(own_field, (2, 0, 1, 3, 4)).reshape(cells)

    edge = jnp.full((1,) + codes.shape[1:], -1, codes.dtype)
    shifted = jnp.concatenate([edge, codes, edge], axis=0)
    shifted = shifted.reshape(slabs + 1, row_count, batch_count, frame_count, across)
    shifted = jnp.transpose(shifted, (0, 3, 1, 2, 4)).reshape(slabs + 1, positions)
    holder = jnp.where(shifted >= 0, shifted // book % planes, -1)

    if whole:
        wanted = lax.dynamic_index_in_dim(shifted, slab_id + section_id, 0, keepdims=False)
        every = lax.all_gather(codebook, SLAB, axis=0, tiled=True)
        taken = jnp.take(every, jnp.maximum(wanted, 0), axis=0)
        pair = jnp.where(wanted[:, None] >= 0, taken, 0).astype(BF16)
    else:
        pair, turned = routed(codebook, shifted, holder, slots, turned)

    place = lax.broadcasted_iota(jnp.int32, (positions, 1), 0)
    group, column = place // across, place % across
    place = (column // row_count) * (positions // slabs) + group * row_count + column % row_count
    sent = (place == lax.broadcasted_iota(jnp.int32, (1, positions), 1)).astype(BF16)
    cotangent = jnp.dot(sent, turned, preferred_element_type=F32).astype(BF16)

    counts = jnp.sum(
        (holder[:, None, :] == lax.broadcasted_iota(jnp.int32, (1, planes, 1), 1)).astype(F32), axis=-1
    )
    crowded = (jnp.max(counts) > slots).astype(F32).reshape(1)

    other = lax.ppermute(pair, "section", [(0, 1), (1, 0)])
    return (
        pair.reshape(cells),
        other.reshape(cells),
        cotangent.reshape(frame_count, -1, channels),
        own,
        crowded,
    )


def line_shares(fields, kernels, codebook, codes, whole):
    section = lax.axis_index("section").reshape(1).astype(jnp.int32)
    slabs = lax.axis_size(SLAB)
    own_field = fields[0]
    kernel = kernels[0]
    row_count, batch_count, frame_count, across, channels = own_field.shape
    pair, other, cotangent, own, crowded = front(own_field, codebook, codes, whole)
    source = shift_source(section, pair, other, across)
    cells = decoder_grad(section, source, kernel, cotangent, own)
    above, below = neighbours(cells[:, -1], cells[:, 0])
    back_dec, pre_act = back_and_forth(section, cells, above, below, kernel, across)
    source = turn_source(section, source, cells, above, below, across)
    returned = lax.ppermute(back_dec, "section", [(1, 0)])

    total = (
        row_count * slabs * across * batch_count * lax.axis_size("dp") * frame_count
    )
    packed = kernel_grads(
        section, source, pre_act, cells, returned, pair, other, lax.axis_size(PLANE)
    )
    plane = exchange(packed, PLANE)
    line = exchange(sum_plane(crowded, plane, lax.axis_size(Z)), Z)
    mark = jnp.max(line[:, -8])
    return exchange(sum_line(line, 1.0 / math.sqrt(total)), Z), mark


def on_device(fields, kernels, codebook, codes):
    line, mark = line_shares(fields, kernels, codebook, codes, False)
    line = lax.cond(
        mark > 0,
        lambda frames, *args: line_shares(*args, True)[0],
        lambda frames, *args: frames,
        line,
        fields,
        kernels,
        codebook,
        codes,
    )
    planes = lax.axis_size(PLANE)
    plane = exchange(spread(line, planes), PLANE)
    return unpack(plane, kernels.shape[-1])[None]


def solution(mesh):
    sections, slabs, dps = (mesh.shape[a] for a in ("section", "slab", "dp"))
    nx = 4 if slabs >= 16 else 2
    inner = Mesh(
        mesh.devices.reshape(sections, slabs // (nx * nx), nx, nx, dps),
        ("section", "zh", "y", "x", "dp"),
    )
    placed = (
        P("section", SLAB, "dp", None, None, None),
        P("section", None, None, None, None, None),
        P(SLAB, None),
        P(None, "dp", None, None),
    )
    return jax.shard_map(
        on_device,
        mesh=inner,
        in_specs=placed,
        out_specs=P("section", None, None, None, None, None),
        check_vma=False,
    )
```
